128 devices in a mesh: pipe: 2 (over core), ctx: 16 (over y, x), dp: 4 (over z).
Axes of the slice: x: 4, y: 4, z: 4, core: 2. Of those that a mesh axis runs over, the one named last changes fastest.
Arguments:
- queries: bfloat16 [2, 4, 2048, 2048], P('pipe', 'dp', 'ctx'), may hold values from -16 to 16
- key_rows: bfloat16 [2, 4, 2048, 512], P('pipe', 'dp', 'ctx'), may hold values from -8 to 8
- layer_value_rows: bfloat16 [2, 4, 2048, 512], P('pipe', 'dp', 'ctx'), may hold values from -6 to 6
- prior_output: bfloat16 [2, 4, 2048, 2048], P('pipe', 'dp', 'ctx'), may hold values from -3 to 3
- later_grad: bfloat16 [2, 4, 2048, 2048], P('pipe', 'dp', 'ctx'), may hold values from -6 to 6
- block_order: int32 [32], replicated, may hold values from 0 to 31, each once
- log_table: float32 [2, 16], P('pipe'), may hold values from 0 to 3
- dim_index: int32 [2, 64], P('pipe'), may hold values from 0 to 15, as said below
Outputs:
- attended: bfloat16 [2, 4, 2048, 2048], P('pipe', 'dp', 'ctx')
- query_gradient: bfloat16 [2, 4, 2048, 2048], P('pipe', 'dp', 'ctx')
- key_gradient: bfloat16 [2, 4, 2048, 512], P('pipe', 'dp', 'ctx')
- value_gradient: bfloat16 [2, 4, 2048, 512], P('pipe', 'dp', 'ctx')
- table_grad: float32 [2, 16], P('pipe')
The draws below stay inside these ranges and needn't reach their ends.
Inputs may be any that keep to these rules, and one draw needn't show every extreme that they name: `block_order`: a permutation. `dim_index`: each row names every table entry equally often.
All inputs are finite; a program needn't handle non-finite values.
Results may differ from the reference program's by a relative error of at most 0.025.
Values may be sent and summed in bfloat16 or wider, within the bound.
No kernel may reach another device: no remote copies, remote signals or barrier semaphores. Data moves between devices by JAX's collectives and lax.ppermute only.
A program may use at most 64 MiB of HBM per device.

```python
import jax
import jax.numpy as jnp
from jax import lax

QUERY_HEADS = 16
KEY_VALUE_HEADS = 4
HEAD_SIZE = 128
NTAB = 16
HALF = 64
QUERY_GROUP = 4
SEQUENCE_TOKENS = 2048
LAYER_COUNT = 2
BATCH_SEQUENCES = 4
N_CTX = 16


def draw_queries(key, part):
    rotary_base = jnp.clip(jax.random.normal(jax.random.fold_in(key, 1), (LAYER_COUNT, BATCH_SEQUENCES, SEQUENCE_TOKENS, KEY_VALUE_HEADS, QUERY_HEADS // KEY_VALUE_HEADS, HEAD_SIZE), jnp.float32), -6.0, 6.0)
    return rotary_base.reshape(LAYER_COUNT, BATCH_SEQUENCES, SEQUENCE_TOKENS, QUERY_HEADS * HEAD_SIZE).astype(jnp.bfloat16)


def draw_key_rows(key, part):
    rotary_base = jnp.clip(jax.random.normal(jax.random.fold_in(key, 2), (LAYER_COUNT, BATCH_SEQUENCES, SEQUENCE_TOKENS, KEY_VALUE_HEADS, HEAD_SIZE), jnp.float32), -6.0, 6.0)
    return rotary_base.reshape(LAYER_COUNT, BATCH_SEQUENCES, SEQUENCE_TOKENS, KEY_VALUE_HEADS * HEAD_SIZE).astype(jnp.bfloat16)


def draw_dim_index(key, part):
    orders = jax.vmap(lambda sub_key: jax.random.permutation(sub_key, HALF))(jax.random.split(key, LAYER_COUNT))
    return (orders % NTAB).astype(jnp.int32)


def level_of(rng, dims, pieces, low, largest):
    loudness = 1.0
    for dim, parts in pieces:
        heights = jax.random.uniform(jax.random.fold_in(jax.random.fold_in(rng, 6), dim), (parts,), jnp.float32, low / len(pieces), largest / len(pieces))
        loudness = loudness * jnp.repeat(jnp.exp(heights), dims[dim] // parts).reshape((-1,) + (1,) * (len(dims) - 1 - dim))
    return loudness


def scatter_about(rng, dims, spread, limit, shards=(), kind=jnp.bfloat16):
    level = level_of(rng, dims, shards, -0.22, 0.18) if shards else 1.0
    drawn = jax.random.normal(rng, dims, jnp.float32) * spread * level
    return jnp.minimum(jnp.maximum(drawn, -limit), limit).astype(kind)


def setup_inputs(seed: int = 0) -> dict:
    arg_keys = jax.random.split(jax.random.key(seed), 9)
    queries = draw_queries(jax.random.fold_in(arg_keys[8], 71), 0)
    key_rows = draw_key_rows(jax.random.fold_in(arg_keys[8], 71), 0)
    layer_value_rows = scatter_about(arg_keys[2], (LAYER_COUNT, BATCH_SEQUENCES, SEQUENCE_TOKENS, KEY_VALUE_HEADS * HEAD_SIZE), 1.0, 6.0, ((0, 2), (1, 4), (2, 16)))
    prior_output = scatter_about(arg_keys[3], (LAYER_COUNT, BATCH_SEQUENCES, SEQUENCE_TOKENS, QUERY_HEADS * HEAD_SIZE), 0.5, 3.0, ((0, 2), (1, 4), (2, 16)))
    later_grad = scatter_about(arg_keys[4], (LAYER_COUNT, BATCH_SEQUENCES, SEQUENCE_TOKENS, QUERY_HEADS * HEAD_SIZE), 1.0, 6.0, ((0, 2), (1, 4), (2, 16)))
    block_order = jax.random.permutation(arg_keys[5], 2 * N_CTX).astype(jnp.int32)
    log_table = jnp.clip(3.0 * jax.random.uniform(arg_keys[6], (LAYER_COUNT, NTAB), jnp.float32) ** level_of(arg_keys[6], (LAYER_COUNT, NTAB), ((0, 2),), -0.2, 0.2), 0.0, 3.0)
    dim_index = draw_dim_index(jax.random.fold_in(arg_keys[8], 71), 0)
    return dict(queries=queries, key_rows=key_rows, layer_value_rows=layer_value_rows, prior_output=prior_output, later_grad=later_grad, block_order=block_order, log_table=log_table, dim_index=dim_index)


neg_large = -1e+30
rope_base = 500000.0

def apply_rotation(vectors, cosine_values, sine_lookup):
    half_len = vectors.shape[-1] // 2
    lower_half = vectors[..., :half_len]
    upper_half = vectors[..., half_len:]
    return jnp.concatenate([lower_half * cosine_values - upper_half * sine_lookup, lower_half * sine_lookup + upper_half * cosine_values], axis=-1)

def rotate_back(gradient, cosine_values, sine_lookup):
    half_len = gradient.shape[-1] // 2
    lower_half = gradient[..., :half_len]
    upper_half = gradient[..., half_len:]
    return jnp.concatenate([lower_half * cosine_values + upper_half * sine_lookup, upper_half * cosine_values - lower_half * sine_lookup], axis=-1)

def angle_grad(gradient, rotated):
    half_len = gradient.shape[-1] // 2
    return lax.optimization_barrier(jnp.sum(gradient[..., half_len:] * rotated[..., :half_len] - gradient[..., :half_len] * rotated[..., half_len:], axis=1))

def angles_for(table_row, index_row, positions, head_dim):
    half_len = head_dim // 2
    onehot = (index_row[:, None] == jnp.arange(table_row.shape[0], dtype=jnp.int32)[None, :]).astype(jnp.float32)
    log_factor = jnp.dot(onehot, table_row, precision=lax.Precision.HIGHEST)
    base_rate = rope_base ** (-(jnp.arange(half_len, dtype=jnp.float32) * 2.0 / head_dim))
    scaled_rate = base_rate * jnp.exp(-log_factor)
    return (onehot, positions[:, None] * scaled_rate[None, :])

def reference(queries, key_rows, layer_value_rows, prior_output, later_grad, block_order, log_table, dim_index):
    half_len = SEQUENCE_TOKENS // (2 * N_CTX)
    positions = (block_order[:, None] * half_len + jnp.arange(half_len, dtype=jnp.int32)[None, :]).reshape(-1).astype(jnp.float32)
    score_scale = HEAD_SIZE ** (-0.5)
    previous = jnp.roll(prior_output, 1, axis=0)
    following = jnp.roll(later_grad, -1, axis=0)
    visible = positions[None, :] <= positions[:, None]
    attended_all, query_all, key_all, value_all, table_all = ([], [], [], [], [])
    for section_number in range(LAYER_COUNT):
        onehot, angles = angles_for(log_table[section_number], dim_index[section_number], positions, HEAD_SIZE)
        cosine_values = jnp.cos(angles)[:, None, :]
        sine_lookup = jnp.sin(angles)[:, None, :]

        def layer_item(items):
            query_row, key_row_item, value_row_item, input_row, gradient_row_item = items
            mixed = (query_row.astype(jnp.float32) + input_row.astype(jnp.float32)).reshape(SEQUENCE_TOKENS, QUERY_HEADS, HEAD_SIZE)
            rotated_query_rows = apply_rotation(mixed, cosine_values, sine_lookup).astype(jnp.bfloat16)
            rotated_key_rows = apply_rotation(key_row_item.astype(jnp.float32).reshape(SEQUENCE_TOKENS, KEY_VALUE_HEADS, HEAD_SIZE), cosine_values, sine_lookup).astype(jnp.bfloat16)
            grouped_queries = rotated_query_rows.reshape(SEQUENCE_TOKENS, KEY_VALUE_HEADS, QUERY_GROUP, HEAD_SIZE).astype(jnp.float32)
            value_head_rows = value_row_item.reshape(SEQUENCE_TOKENS, KEY_VALUE_HEADS, HEAD_SIZE).astype(jnp.float32)
            keys_float = rotated_key_rows.astype(jnp.float32)
            scores = jnp.einsum('qhgd,khd->hgqk', grouped_queries, keys_float) * score_scale
            row_max = lax.optimization_barrier(jnp.max(jnp.where(visible, scores, neg_large), axis=-1))
            weights = jnp.where(visible, jnp.exp(scores - row_max[..., None]), 0.0)
            totals = lax.optimization_barrier(jnp.sum(weights, axis=-1))
            summed = jnp.einsum('hgqk,khd->qhgd', weights.astype(jnp.bfloat16).astype(jnp.float32), value_head_rows)
            final_result = (summed / jnp.moveaxis(totals, -1, 0)[..., None]).astype(jnp.bfloat16)
            log_totals = row_max + jnp.log(totals)
            output_gradient = gradient_row_item.reshape(SEQUENCE_TOKENS, KEY_VALUE_HEADS, QUERY_GROUP, HEAD_SIZE).astype(jnp.float32)
            row_delta = jnp.moveaxis(lax.optimization_barrier(jnp.sum(output_gradient * final_result.astype(jnp.float32), axis=-1)), 0, -1)
            probs = jnp.where(visible, jnp.exp(scores - log_totals[..., None]), 0.0)
            value_gradient = jnp.einsum('hgqk,qhgd->khd', probs.astype(jnp.bfloat16).astype(jnp.float32), output_gradient)
            prob_grad = jnp.einsum('qhgd,khd->hgqk', output_gradient, value_head_rows)
            score_grad = (probs * (prob_grad - row_delta[..., None])).astype(jnp.bfloat16).astype(jnp.float32)
            query_rot_grad = jnp.einsum('hgqk,khd->qhgd', score_grad, keys_float) * score_scale
            key_rot_grad = jnp.einsum('hgqk,qhgd->khd', score_grad, grouped_queries) * score_scale
            query_rot_grad = query_rot_grad.reshape(SEQUENCE_TOKENS, QUERY_HEADS, HEAD_SIZE)
            query_gradient = rotate_back(query_rot_grad, cosine_values, sine_lookup).astype(jnp.bfloat16)
            key_gradient = rotate_back(key_rot_grad, cosine_values, sine_lookup).astype(jnp.bfloat16)
            angle_sums = angle_grad(query_rot_grad, rotated_query_rows.astype(jnp.float32)) + angle_grad(key_rot_grad, keys_float)
            log_gradient = -lax.optimization_barrier(jnp.sum(angle_sums * angles, axis=0))
            return (final_result.reshape(SEQUENCE_TOKENS, QUERY_HEADS * HEAD_SIZE), query_gradient.reshape(SEQUENCE_TOKENS, QUERY_HEADS * HEAD_SIZE), key_gradient.reshape(SEQUENCE_TOKENS, KEY_VALUE_HEADS * HEAD_SIZE), value_gradient.astype(jnp.bfloat16).reshape(SEQUENCE_TOKENS, KEY_VALUE_HEADS * HEAD_SIZE), log_gradient)
        results = lax.map(layer_item, (queries[section_number], key_rows[section_number], layer_value_rows[section_number], previous[section_number], following[section_number]))
        attended_all.append(results[0])
        query_all.append(results[1])
        key_all.append(results[2])
        value_all.append(results[3])
        log_gradient = lax.optimization_barrier(jnp.sum(results[4], axis=0)) / (BATCH_SEQUENCES * SEQUENCE_TOKENS)
        table_all.append(jnp.dot(log_gradient, onehot, precision=lax.Precision.HIGHEST))
    return (jnp.stack(attended_all), jnp.stack(query_all), jnp.stack(key_all), jnp.stack(value_all), jnp.stack(table_all))
```

```python
import functools
import math

import jax
import jax.numpy as jnp
from jax import lax
from jax.experimental import pallas as pl
from jax.experimental.pallas import tpu as pltpu
from jax.sharding import PartitionSpec as P

HEAD = 128
HALF = 64
ROPE_BASE = 500000.0
LOG_ROWS = 16
TILE = 256
LOG2E = math.log2(math.e)

VMEM = pl.BlockSpec(memory_space=pltpu.VMEM)
SMEM = pl.BlockSpec(memory_space=pltpu.SMEM)
f32 = jnp.float32
bf16 = jnp.bfloat16


def dot(a, b):
    return jnp.dot(a, b, preferred_element_type=f32)


def dot_nt(a, b):
    return lax.dot_general(a, b, (((1,), (1,)), ((), ())), preferred_element_type=f32)


def swap_halves(u):
    return pltpu.roll(u, HALF, 1)


def lane_rates(table_ref, index_row):
    lane = lax.broadcasted_iota(jnp.int32, (1, HEAD), 1)
    pair = jnp.where(lane < HALF, lane, lane - HALF).astype(f32)
    log_factor = jnp.zeros((1, HEAD), f32)
    for entry in range(table_ref.shape[1]):
        log_factor = jnp.where(index_row == entry, table_ref[0, entry], log_factor)
    return jnp.exp(-pair * (2.0 / HEAD * math.log(ROPE_BASE)) - log_factor)


def before_kernel(order_ref, table_ref, index_ref, q_ref, prior_ref, k_ref, v_ref, do_ref,
                  out_ref, cos_ref, sin_ref):
    rows = q_ref.shape[0]
    half_rows = rows // 2
    heads = q_ref.shape[1] // HEAD
    group = q_ref.shape[1] // k_ref.shape[1]
    me = lax.axis_index("ctx")
    rate = lane_rates(table_ref, index_ref[...])
    row = lax.broadcasted_iota(jnp.int32, (rows, HEAD), 0)
    first, second = order_ref[2 * me] * half_rows, order_ref[2 * me + 1] * half_rows
    position = jnp.where(row < half_rows, first + row, second + row - half_rows).astype(f32)
    angle = position * rate
    lane = lax.broadcasted_iota(jnp.int32, (rows, HEAD), 1)
    cosine = jnp.cos(angle)
    sine = jnp.sin(angle)
    signed = jnp.where(lane < HALF, -sine, sine)
    cos_ref[...] = cosine
    sin_ref[...] = signed
    rotated_keys = []
    for head in range(heads // group):
        cols = slice(head * HEAD, (head + 1) * HEAD)
        u = k_ref[:, cols].astype(f32)
        rotated_keys.append((u * cosine + swap_halves(u) * signed).astype(bf16))
    for head in range(heads):
        cols = slice(head * HEAD, (head + 1) * HEAD)
        u = q_ref[:, cols].astype(f32) + prior_ref[:, cols].astype(f32)
        out_ref[head, 0:rows] = (u * cosine + swap_halves(u) * signed).astype(bf16)
        out_ref[head, rows:2 * rows] = do_ref[:, cols]
        out_ref[head, 2 * rows:3 * rows] = rotated_keys[head // group]
        kv = head // group
        out_ref[head, 3 * rows:4 * rows] = v_ref[:, kv * HEAD:(kv + 1) * HEAD]


def main_kernel(order_ref, in_ref, out_ref, qs, dos, ks, vs, kt, vt, dk, dv, atts, dqs, s_scr, e_scr, ds_scr):
    sources = in_ref.shape[0]
    rows = in_ref.shape[1] // 4
    half_rows = rows // 2
    tokens = sources * rows
    tiles = tokens // TILE
    scale = HEAD ** -0.5
    coef = scale * LOG2E

    for slot in range(2 * sources):
        to = pl.ds(pl.multiple_of(order_ref[slot] * half_rows, half_rows), half_rows)
        for number, ref in enumerate((qs, dos, ks, vs)):
            start = number * rows + (slot % 2) * half_rows
            ref[to, :] = in_ref[slot // 2, start:start + half_rows, :]
    kt[...] = ks[...].T
    vt[...] = vs[...].T

    key_iota = lax.broadcasted_iota(jnp.int32, (TILE, TILE), 0)
    query_iota = lax.broadcasted_iota(jnp.int32, (TILE, TILE), 1)
    visible = key_iota <= query_iota
    row_number = lax.broadcasted_iota(jnp.int32, (TILE, HEAD), 0)
    angle_sum = jnp.zeros((8, HEAD), f32)

    def weighted(gradient, rotated, base):
        term = gradient * swap_halves(rotated.astype(f32)) * (row_number + base).astype(f32)
        return jnp.sum(term.reshape(TILE // 8, 8, HEAD), axis=0)

    for i in range(tiles):
        tile = slice(i * TILE, (i + 1) * TILE)
        seen = (i + 1) * TILE
        q = qs[tile, :]
        do_t = dos[tile, :].T.astype(f32)
        top = None
        for c in range(i + 1):
            keys = slice(c * TILE, (c + 1) * TILE)
            s = dot_nt(ks[keys, :], q)
            if c == i:
                s = jnp.where(visible, s, -1e30)
            s_scr[keys, :] = s
            high = jnp.max(s, axis=0, keepdims=True)
            top = high if top is None else jnp.maximum(top, high)
        top = top * coef
        total = jnp.zeros((1, TILE), f32)
        for c in range(i + 1):
            keys = slice(c * TILE, (c + 1) * TILE)
            e = jnp.exp2(s_scr[keys, :] * coef - top)
            total = total + jnp.sum(e, axis=0, keepdims=True)
            e_scr[keys, :] = e.astype(bf16)
        inverse = 1.0 / total
        o_t = dot(vt[:, :seen], e_scr[:seen, :]) * inverse
        atts[tile, :] = o_t.T.astype(bf16)
        do_t = (do_t * inverse).astype(bf16)
        delta = jnp.sum(do_t.astype(f32) * o_t, axis=0, keepdims=True)
        do = do_t.T
        for c in range(i + 1):
            keys = slice(c * TILE, (c + 1) * TILE)
            e = e_scr[keys, :]
            value_part = dot(e, do)
            dp = dot(vs[keys, :], do_t)
            ds = (e.astype(f32) * (dp - delta)).astype(bf16)
            ds_scr[keys, :] = ds
            key_part = dot(ds, q)
            if c == i:
                dv[keys, :] = value_part
                dk[keys, :] = key_part
            else:
                dv[keys, :] += value_part
                dk[keys, :] += key_part
        gq = (dot(kt[:, :seen], ds_scr[:seen, :]) * scale).T
        dqs[tile, :] = gq.astype(bf16)
        angle_sum = angle_sum + weighted(gq, q, i * TILE)

    for i in range(tiles):
        tile = slice(i * TILE, (i + 1) * TILE)
        gk = dk[tile, :] * scale
        dk[tile, :] = gk
        angle_sum = angle_sum + weighted(gk, ks[tile, :], i * TILE)

    for slot in range(2 * sources):
        at = pl.ds(pl.multiple_of(order_ref[slot] * half_rows, half_rows), half_rows)
        for number, ref in enumerate((atts, dqs, dk, dv)):
            start = number * rows + (slot % 2) * half_rows
            out_ref[slot // 2, start:start + half_rows, :] = ref[at, :].astype(bf16)
    line = jnp.sum(angle_sum, axis=0, keepdims=True)
    high = line.astype(bf16).astype(f32)
    middle = (line - high).astype(bf16).astype(f32)
    low = line - high - middle
    which = lax.broadcasted_iota(jnp.int32, (LOG_ROWS, HEAD), 0)
    packed = jnp.where(which == 0, high, jnp.where(which == 1, middle, jnp.where(which == 2, low, 0.0)))
    for source in range(sources):
        out_ref[source, 4 * rows:, :] = packed.astype(bf16)


def after_kernel(in_ref, cos_ref, sin_ref, att_ref, dq_ref, dk_ref, dv_ref):
    rows = cos_ref.shape[0]
    heads = in_ref.shape[0]
    group = att_ref.shape[1] // dk_ref.shape[1]
    cosine, signed = cos_ref[...], sin_ref[...]

    def back(u):
        return (u * cosine - swap_halves(u) * signed).astype(bf16)

    for kv in range(heads // group):
        key_sum = jnp.zeros((rows, HEAD), f32)
        value_sum = jnp.zeros((rows, HEAD), f32)
        for head in range(kv * group, (kv + 1) * group):
            cols = slice(head * HEAD, (head + 1) * HEAD)
            att_ref[:, cols] = in_ref[head, 0:rows]
            dq_ref[:, cols] = back(in_ref[head, rows:2 * rows].astype(f32))
            key_sum = key_sum + in_ref[head, 2 * rows:3 * rows].astype(f32)
            value_sum = value_sum + in_ref[head, 3 * rows:4 * rows].astype(f32)
        cols = slice(kv * HEAD, (kv + 1) * HEAD)
        dk_ref[:, cols] = back(key_sum)
        dv_ref[:, cols] = value_sum.astype(bf16)


def shape(*dims, dtype=bf16):
    return jax.ShapeDtypeStruct(dims, dtype)


def on_device(queries, key_rows, values, prior, later, order, table, index):
    rows, width = queries.shape[2:]
    kv_width = key_rows.shape[3]
    heads = width // HEAD
    sources = lax.axis_size("ctx")
    pipe = lax.axis_size("pipe")
    tokens = rows * sources
    arriving = lax.ppermute(prior, "pipe", [(i, (i + 1) % pipe) for i in range(pipe)])
    returning = lax.ppermute(later, "pipe", [(i, (i - 1) % pipe) for i in range(pipe)])
    wide_index = jnp.concatenate([index, index], axis=1)
    params = pltpu.CompilerParams(vmem_limit_bytes=40 * 2**20)

    sent, cosine, sine = pl.pallas_call(
        before_kernel,
        out_shape=(shape(heads, 4 * rows, HEAD), shape(rows, HEAD, dtype=f32), shape(rows, HEAD, dtype=f32)),
        in_specs=[SMEM, SMEM] + [VMEM] * 6,
        out_specs=[VMEM] * 3,
        compiler_params=params,
    )(order, table, wide_index, queries[0, 0], arriving[0, 0], key_rows[0, 0], values[0, 0], returning[0, 0])

    held = lax.all_to_all(sent, "ctx", 0, 0)

    done = pl.pallas_call(
        main_kernel,
        out_shape=shape(sources, 4 * rows + LOG_ROWS, HEAD),
        in_specs=[SMEM, VMEM],
        out_specs=VMEM,
        scratch_shapes=[pltpu.VMEM((tokens, HEAD), bf16)] * 4
        + [pltpu.VMEM((HEAD, tokens), bf16)] * 2
        + [pltpu.VMEM((tokens, HEAD), f32)] * 2
        + [pltpu.VMEM((tokens, HEAD), bf16)] * 2
        + [pltpu.VMEM((tokens, TILE), f32)]
        + [pltpu.VMEM((tokens, TILE), bf16)] * 2,
        compiler_params=params,
    )(order, held)

    back = lax.all_to_all(done, "ctx", 0, 0)

    line = jnp.sum(back[:, 4 * rows:4 * rows + 3, :].astype(f32), axis=(0, 1))
    dp = lax.axis_size("dp")
    terms = [lax.ppermute(line, "dp", [(i, i ^ s) for i in range(dp)]) for s in range(1, dp)]

    attended, dq, dk, dv = pl.pallas_call(
        after_kernel,
        out_shape=(shape(rows, width), shape(rows, width), shape(rows, kv_width), shape(rows, kv_width)),
        in_specs=[VMEM] * 3,
        out_specs=[VMEM] * 4,
        compiler_params=params,
    )(back, cosine, sine)

    level = [line] + terms
    while len(level) > 1:
        level = [a + b for a, b in zip(level[0::2], level[1::2])]
    line = level[0]
    base = ROPE_BASE ** (-(jnp.arange(HALF, dtype=f32) * 2.0 / HEAD))
    onehot = (index[0][:, None] == jnp.arange(table.shape[1], dtype=jnp.int32)[None, :]).astype(f32)
    log_factor = jnp.sum(onehot * table[0][None, :], axis=1)
    log_gradient = (line[:HALF] - line[HALF:]) * base * jnp.exp(-log_factor)
    table_grad = jnp.sum(onehot * log_gradient[:, None], axis=0) / (tokens * dp)
    return attended[None, None], dq[None, None], dk[None, None], dv[None, None], table_grad[None, :]


def solution(mesh):
    block = P("pipe", "dp", "ctx", None)
    return jax.shard_map(
        on_device,
        mesh=mesh,
        in_specs=(block,) * 5 + (P(), P("pipe", None), P("pipe", None)),
        out_specs=(block,) * 4 + (P("pipe", None),),
        check_vma=False,
    )
```

```python
import math

import jax
import jax.numpy as jnp
from jax import lax
from jax.experimental import pallas as pl
from jax.experimental.pallas import tpu as pltpu
from jax.sharding import PartitionSpec as P

HEAD = 128
HALF = 64
ROPE_BASE = 500000.0
TILE = 256
LOG2E = math.log2(math.e)

VMEM = pl.BlockSpec(memory_space=pltpu.VMEM)
SMEM = pl.BlockSpec(memory_space=pltpu.SMEM)
ANY = pl.BlockSpec(memory_space=pl.ANY)
HBM = pl.BlockSpec(memory_space=pltpu.HBM)
f32 = jnp.float32
bf16 = jnp.bfloat16


def dot(a, b):
    return jnp.dot(a, b, preferred_element_type=f32)


def dot_nt(a, b):
    return lax.dot_general(a, b, (((1,), (1,)), ((), ())), preferred_element_type=f32)


def swap_halves(u):
    return pltpu.roll(u, HALF, 1)


def half_rates(table_ref, index_row):
    pair = lax.broadcasted_iota(jnp.int32, (1, HALF), 1).astype(f32)
    log_factor = jnp.zeros((1, HALF), f32)
    for entry in range(table_ref.shape[1]):
        log_factor = jnp.where(index_row == entry, table_ref[0, entry], log_factor)
    return jnp.exp(-pair * (2.0 / HEAD * math.log(ROPE_BASE)) - log_factor)


def first_kernel(order_hbm, table_hbm, index_hbm, q_hbm, k_hbm, v_hbm,
                 out_ref, cos_ref, sin_ref, q_ref,
                 order_ref, table_ref, index_ref, k_ref, v_ref, sems):
    pairs = ((order_hbm, order_ref), (table_hbm, table_ref), (index_hbm, index_ref),
             (k_hbm, k_ref), (v_hbm, v_ref), (q_hbm, q_ref))
    copies = [pltpu.make_async_copy(a, b, sems.at[i]) for i, (a, b) in enumerate(pairs)]
    for copy in copies:
        copy.start()
    for copy in copies[:3]:
        copy.wait()
    rows = q_ref.shape[0]
    half_rows = rows // 2
    heads = q_ref.shape[1] // HEAD
    group = q_ref.shape[1] // k_ref.shape[1]
    me = lax.axis_index("ctx")
    rate = half_rates(table_ref, index_ref[...])
    row = lax.broadcasted_iota(jnp.int32, (rows, HALF), 0)
    first, second = order_ref[2 * me] * half_rows, order_ref[2 * me + 1] * half_rows
    position = jnp.where(row < half_rows, first + row, second + row - half_rows).astype(f32)
    angle = position * rate
    cosine = jnp.cos(angle)
    sine = jnp.sin(angle)
    cosine = jnp.concatenate([cosine, cosine], axis=1)
    signed = jnp.concatenate([-sine, sine], axis=1)
    cos_ref[...] = cosine
    sin_ref[...] = signed
    copies[3].wait()
    copies[4].wait()
    for kv in range(heads // group):
        cols = slice(kv * HEAD, (kv + 1) * HEAD)
        u = k_ref[:, cols].astype(f32)
        rotated = (u * cosine + swap_halves(u) * signed).astype(bf16)
        value = v_ref[:, cols]
        for head in range(kv * group, (kv + 1) * group):
            out_ref[head, 2 * rows:3 * rows] = rotated
            out_ref[head, 3 * rows:4 * rows] = value
    copies[5].wait()


def second_kernel(held_ref, q_ref, cos_ref, sin_ref, prior_ref, do_ref, out_ref):
    rows = q_ref.shape[0]
    heads = q_ref.shape[1] // HEAD
    cosine, signed = cos_ref[...], sin_ref[...]
    for head in range(heads):
        cols = slice(head * HEAD, (head + 1) * HEAD)
        u = q_ref[:, cols].astype(f32) + prior_ref[:, cols].astype(f32)
        out_ref[head, 0:rows] = (u * cosine + swap_halves(u) * signed).astype(bf16)
        out_ref[head, rows:2 * rows] = do_ref[:, cols]


def main_kernel(order_ref, in_ref, out_ref, line_ref, qs, dos, ks, vs, kt, vt, dk, dv, atts, dqs, s_scr, e_scr, ds_scr):
    sources = in_ref.shape[0]
    rows = in_ref.shape[1] // 4
    half_rows = rows // 2
    tokens = sources * rows
    tiles = tokens // TILE
    scale = HEAD ** -0.5
    coef = scale * LOG2E

    for slot in range(2 * sources):
        to = pl.ds(pl.multiple_of(order_ref[slot] * half_rows, half_rows), half_rows)
        for number, ref in enumerate((qs, dos, ks, vs)):
            start = number * rows + (slot % 2) * half_rows
            ref[to, :] = in_ref[slot // 2, start:start + half_rows, :]
    kt[...] = ks[...].T
    vt[...] = vs[...].T

    key_iota = lax.broadcasted_iota(jnp.int32, (TILE, TILE), 0)
    query_iota = lax.broadcasted_iota(jnp.int32, (TILE, TILE), 1)
    visible = key_iota <= query_iota
    row_number = lax.broadcasted_iota(jnp.int32, (TILE, HEAD), 0)
    angle_sum = jnp.zeros((8, HEAD), f32)

    def weighted(gradient, rotated, base):
        term = gradient * swap_halves(rotated.astype(f32)) * (row_number + base).astype(f32)
        return jnp.sum(term.reshape(TILE // 8, 8, HEAD), axis=0)

    for i in range(tiles):
        tile = slice(i * TILE, (i + 1) * TILE)
        seen = (i + 1) * TILE
        q = qs[tile, :]
        do_t = dos[tile, :].T.astype(f32)
        top = None
        for c in range(i + 1):
            keys = slice(c * TILE, (c + 1) * TILE)
            s = dot_nt(ks[keys, :], q)
            if c == i:
                s = jnp.where(visible, s, -1e30)
            s_scr[keys, :] = s
            high = jnp.max(s, axis=0, keepdims=True)
            top = high if top is None else jnp.maximum(top, high)
        top = top * coef
        total = jnp.zeros((1, TILE), f32)
        for c in range(i + 1):
            keys = slice(c * TILE, (c + 1) * TILE)
            e = jnp.exp2(s_scr[keys, :] * coef - top)
            total = total + jnp.sum(e, axis=0, keepdims=True)
            e_scr[keys, :] = e.astype(bf16)
        inverse = 1.0 / total
        o_t = dot(vt[:, :seen], e_scr[:seen, :]) * inverse
        atts[tile, :] = o_t.T.astype(bf16)
        do_t = (do_t * inverse).astype(bf16)
        delta = jnp.sum(do_t.astype(f32) * o_t, axis=0, keepdims=True)
        do = do_t.T
        for c in range(i + 1):
            keys = slice(c * TILE, (c + 1) * TILE)
            e = e_scr[keys, :]
            value_part = dot(e, do)
            dp = dot(vs[keys, :], do_t)
            ds = (e.astype(f32) * (dp - delta)).astype(bf16)
            ds_scr[keys, :] = ds
            key_part = dot(ds, q)
            if c == i:
                dv[keys, :] = value_part
                dk[keys, :] = key_part
            else:
                dv[keys, :] += value_part
                dk[keys, :] += key_part
        gq = (dot(kt[:, :seen], ds_scr[:seen, :]) * scale).T
        dqs[tile, :] = gq.astype(bf16)
        angle_sum = angle_sum + weighted(gq, q, i * TILE)

    for i in range(tiles):
        tile = slice(i * TILE, (i + 1) * TILE)
        gk = dk[tile, :] * scale
        dk[tile, :] = gk
        angle_sum = angle_sum + weighted(gk, ks[tile, :], i * TILE)

    for slot in range(2 * sources):
        at = pl.ds(pl.multiple_of(order_ref[slot] * half_rows, half_rows), half_rows)
        for number, ref in enumerate((atts, dqs, dk, dv)):
            start = number * rows + (slot % 2) * half_rows
            out_ref[slot // 2, start:start + half_rows, :] = ref[at, :].astype(bf16)
    line = jnp.sum(angle_sum, axis=0, keepdims=True)
    line_ref[...] = jnp.broadcast_to(line, line_ref.shape)


def after_kernel(in_ref, cos_ref, sin_ref, att_ref, dq_ref, dk_ref, dv_ref):
    rows = cos_ref.shape[0]
    heads = in_ref.shape[0]
    group = att_ref.shape[1] // dk_ref.shape[1]
    cosine, signed = cos_ref[...], sin_ref[...]

    def back(u):
        return (u * cosine - swap_halves(u) * signed).astype(bf16)

    for kv in range(heads // group):
        key_sum = jnp.zeros((rows, HEAD), f32)
        value_sum = jnp.zeros((rows, HEAD), f32)
        for head in range(kv * group, (kv + 1) * group):
            cols = slice(head * HEAD, (head + 1) * HEAD)
            att_ref[:, cols] = in_ref[head, 0:rows]
            dq_ref[:, cols] = back(in_ref[head, rows:2 * rows].astype(f32))
            key_sum = key_sum + in_ref[head, 2 * rows:3 * rows].astype(f32)
            value_sum = value_sum + in_ref[head, 3 * rows:4 * rows].astype(f32)
        cols = slice(kv * HEAD, (kv + 1) * HEAD)
        dk_ref[:, cols] = back(key_sum)
        dv_ref[:, cols] = value_sum.astype(bf16)


def shape(*dims, dtype=bf16):
    return jax.ShapeDtypeStruct(dims, dtype)


def added_up(value, axis, size, stride):
    devices = range(lax.axis_size(axis))
    level = [value] + [lax.ppermute(value, axis, [(i, i ^ (s * stride)) for i in devices]) for s in range(1, size)]
    while len(level) > 1:
        level = [a + b for a, b in zip(level[0::2], level[1::2])]
    return level[0]


def on_device(queries, key_rows, values, prior, later, order, table, index):
    rows, width = queries.shape[2:]
    kv_width = key_rows.shape[3]
    heads = width // HEAD
    sources = lax.axis_size("ctx")
    pipe = lax.axis_size("pipe")
    tokens = rows * sources
    arriving = lax.ppermute(prior, "pipe", [(i, (i + 1) % pipe) for i in range(pipe)])
    returning = lax.ppermute(later, "pipe", [(i, (i - 1) % pipe) for i in range(pipe)])
    params = pltpu.CompilerParams(vmem_limit_bytes=40 * 2**20)
    payload = shape(heads, 4 * rows, HEAD)
    wave = shape(rows, HEAD, dtype=f32)

    partly, cosine, sine, own = pl.pallas_call(
        first_kernel,
        out_shape=(payload, wave, wave, shape(rows, width)),
        in_specs=[HBM] * 6,
        out_specs=[VMEM] * 4,
        scratch_shapes=[
            pltpu.SMEM(order.shape, jnp.int32),
            pltpu.SMEM(table.shape, f32),
            pltpu.VMEM(index.shape, jnp.int32),
            pltpu.VMEM((rows, kv_width), bf16),
            pltpu.VMEM((rows, kv_width), bf16),
            pltpu.SemaphoreType.DMA((6,)),
        ],
        compiler_params=pltpu.CompilerParams(vmem_limit_bytes=56 * 2**20),
        cost_estimate=pl.CostEstimate(flops=10**7, bytes_accessed=4 * 10**6, transcendentals=0),
    )(order, table, index, queries[0, 0], key_rows[0, 0], values[0, 0])

    sent = pl.pallas_call(
        second_kernel,
        out_shape=payload,
        in_specs=[ANY] + [VMEM] * 5,
        out_specs=VMEM,
        input_output_aliases={0: 0},
        compiler_params=params,
    )(partly, own, cosine, sine, arriving[0, 0], returning[0, 0])

    held = lax.all_to_all(sent, "ctx", 0, 0)

    dp = lax.axis_size("dp")
    done, line = pl.pallas_call(
        main_kernel,
        out_shape=(payload, shape(8, HEAD, dtype=f32)),
        in_specs=[SMEM, VMEM],
        out_specs=[VMEM, VMEM],
        scratch_shapes=[pltpu.VMEM((tokens, HEAD), bf16)] * 4
        + [pltpu.VMEM((HEAD, tokens), bf16)] * 2
        + [pltpu.VMEM((tokens, HEAD), f32)] * 2
        + [pltpu.VMEM((tokens, HEAD), bf16)] * 2
        + [pltpu.VMEM((tokens, TILE), f32)]
        + [pltpu.VMEM((tokens, TILE), bf16)] * 2,
        compiler_params=params,
    )(order, held)

    back = lax.all_to_all(done, "ctx", 0, 0)
    line = added_up(line, "dp", dp, 1)
    line = added_up(line, "ctx", 4, 1)
    line = added_up(line, "ctx", sources // 4, 4)

    attended, dq, dk, dv = pl.pallas_call(
        after_kernel,
        out_shape=(shape(rows, width), shape(rows, width), shape(rows, kv_width), shape(rows, kv_width)),
        in_specs=[VMEM] * 3,
        out_specs=[VMEM] * 4,
        compiler_params=params,
    )(back, cosine, sine)

    line = line[0]
    base = ROPE_BASE ** (-(jnp.arange(HALF, dtype=f32) * 2.0 / HEAD))
    onehot = (index[0][:, None] == jnp.arange(table.shape[1], dtype=jnp.int32)[None, :]).astype(f32)
    log_factor = jnp.sum(onehot * table[0][None, :], axis=1)
    log_gradient = (line[:HALF] - line[HALF:]) * base * jnp.exp(-log_factor)
    table_grad = jnp.sum(onehot * log_gradient[:, None], axis=0) / (tokens * dp)
    return attended[None, None], dq[None, None], dk[None, None], dv[None, None], table_grad[None, :]


def solution(mesh):
    block = P("pipe", "dp", "ctx", None)
    return jax.shard_map(
        on_device,
        mesh=mesh,
        in_specs=(block,) * 5 + (P(), P("pipe", None), P("pipe", None)),
        out_specs=(block,) * 4 + (P("pipe", None),),
        check_vma=False,
    )
```

```python
import math

import jax
import jax.numpy as jnp
from jax import lax
from jax.experimental import pallas as pl
from jax.experimental.pallas import tpu as pltpu
from jax.sharding import PartitionSpec as P

HEAD = 128
HALF = 64
ROPE_BASE = 500000.0
LOG_ROWS = 16
TILE = 512
LOG2E = math.log2(math.e)

VMEM = pl.BlockSpec(memory_space=pltpu.VMEM)
SMEM = pl.BlockSpec(memory_space=pltpu.SMEM)
HBM = pl.BlockSpec(memory_space=pltpu.HBM)
f32 = jnp.float32
bf16 = jnp.bfloat16


def dot(a, b):
    return jnp.dot(a, b, preferred_element_type=f32)


def dot_nt(a, b):
    return lax.dot_general(a, b, (((1,), (1,)), ((), ())), preferred_element_type=f32)


def swap_halves(u):
    return pltpu.roll(u, HALF, 1)


def half_rates(table_ref, index_row):
    pair = lax.broadcasted_iota(jnp.int32, (1, HALF), 1).astype(f32)
    log_factor = jnp.zeros((1, HALF), f32)
    for entry in range(table_ref.shape[1]):
        log_factor = jnp.where(index_row == entry, table_ref[0, entry], log_factor)
    return jnp.exp(-pair * (2.0 / HEAD * math.log(ROPE_BASE)) - log_factor)


def before_kernel(order_hbm, table_hbm, index_hbm, q_hbm, k_hbm, v_hbm, prior_hbm, do_hbm,
                  out_hbm, cos_hbm, sin_hbm,
                  order_ref, table_ref, index_ref, q_ref, k_ref, prior_ref, do_ref, v_ref, packed_q, packed_k, cos_ref, sin_ref,
                  in_sems, do_sems, v_sems, q_sems, k_sems, wave_sems):
    rows, width = q_ref.shape
    half_rows = rows // 2
    heads = width // HEAD
    group = width // k_ref.shape[1]
    pairs = ((order_hbm, order_ref), (table_hbm, table_ref), (index_hbm, index_ref),
             (k_hbm, k_ref), (q_hbm, q_ref), (prior_hbm, prior_ref), (do_hbm, do_ref), (v_hbm, v_ref))
    copies = [pltpu.make_async_copy(a, b, in_sems.at[i]) for i, (a, b) in enumerate(pairs)]
    for copy in copies:
        copy.start()
    sent = []

    def send(source, head, part, sem):
        copy = pltpu.make_async_copy(source, out_hbm.at[head, pl.ds(part * rows, rows), :], sem)
        copy.start()
        sent.append(copy)

    for copy in copies[:3]:
        copy.wait()
    me = lax.axis_index("ctx")
    rate = half_rates(table_ref, index_ref[...])
    row = lax.broadcasted_iota(jnp.int32, (rows, HALF), 0)
    first, second = order_ref[2 * me] * half_rows, order_ref[2 * me + 1] * half_rows
    position = jnp.where(row < half_rows, first + row, second + row - half_rows).astype(f32)
    angle = position * rate
    cosine = jnp.cos(angle)
    sine = jnp.sin(angle)
    cosine = jnp.concatenate([cosine, cosine], axis=1)
    signed = jnp.concatenate([-sine, sine], axis=1)
    cos_ref[...] = cosine
    sin_ref[...] = signed
    for number, (a, b) in enumerate(((cos_ref, cos_hbm), (sin_ref, sin_hbm))):
        copy = pltpu.make_async_copy(a, b, wave_sems.at[number])
        copy.start()
        sent.append(copy)
    copies[6].wait()
    copies[7].wait()
    for head in range(heads):
        send(do_ref.at[:, pl.ds(head * HEAD, HEAD)], head, 1, do_sems.at[head])
        send(v_ref.at[:, pl.ds(head // group * HEAD, HEAD)], head, 3, v_sems.at[head])
    copies[3].wait()
    for kv in range(heads // group):
        u = k_ref[:, kv * HEAD:(kv + 1) * HEAD].astype(f32)
        packed_k[kv] = (u * cosine + swap_halves(u) * signed).astype(bf16)
        for head in range(kv * group, (kv + 1) * group):
            send(packed_k.at[kv], head, 2, k_sems.at[head])
    copies[4].wait()
    copies[5].wait()
    for head in range(heads):
        cols = slice(head * HEAD, (head + 1) * HEAD)
        u = q_ref[:, cols].astype(f32) + prior_ref[:, cols].astype(f32)
        packed_q[head] = (u * cosine + swap_halves(u) * signed).astype(bf16)
        send(packed_q.at[head], head, 0, q_sems.at[head])
    for copy in sent:
        copy.wait()


def main_kernel(order_ref, in_ref, out_ref, qs, dos, ks, vs, kt, vt, dk, dv, atts, dqs, s_scr, e_scr, ds_scr):
    sources = in_ref.shape[0]
    rows = in_ref.shape[1] // 4
    half_rows = rows // 2
    tokens = sources * rows
    tiles = tokens // TILE
    scale = HEAD ** -0.5
    coef = scale * LOG2E

    for slot in range(2 * sources):
        to = pl.ds(pl.multiple_of(order_ref[slot] * half_rows, half_rows), half_rows)
        for number, ref in enumerate((qs, dos, ks, vs)):
            start = number * rows + (slot % 2) * half_rows
            ref[to, :] = in_ref[slot // 2, start:start + half_rows, :]
    kt[...] = ks[...].T
    vt[...] = vs[...].T

    key_iota = lax.broadcasted_iota(jnp.int32, (TILE, TILE), 0)
    query_iota = lax.broadcasted_iota(jnp.int32, (TILE, TILE), 1)
    visible = key_iota <= query_iota
    row_number = lax.broadcasted_iota(jnp.int32, (TILE, HEAD), 0)
    angle_sum = jnp.zeros((8, HEAD), f32)

    def weighted(gradient, rotated, base):
        term = gradient * swap_halves(rotated.astype(f32)) * (row_number + base).astype(f32)
        return jnp.sum(term.reshape(TILE // 8, 8, HEAD), axis=0)

    kept = {}

    def scores(i):
        tile = slice(i * TILE, (i + 1) * TILE)
        q = qs[tile, :]
        top = None
        for c in range(i + 1):
            keys = slice(c * TILE, (c + 1) * TILE)
            s = dot_nt(ks[keys, :], q)
            if c == i:
                s = jnp.where(visible, s, -1e30)
            s_scr[i % 2, keys, :] = s
            high = jnp.max(s, axis=0, keepdims=True)
            top = high if top is None else jnp.maximum(top, high)
        kept[i] = top * coef

    def forward(i):
        tile = slice(i * TILE, (i + 1) * TILE)
        seen = (i + 1) * TILE
        top = kept[i]
        total = jnp.zeros((1, TILE), f32)
        for c in range(i + 1):
            keys = slice(c * TILE, (c + 1) * TILE)
            e = jnp.exp2(s_scr[i % 2, keys, :] * coef - top)
            total = total + jnp.sum(e, axis=0, keepdims=True)
            e_scr[i % 2, keys, :] = e.astype(bf16)
        inverse = 1.0 / total
        o_t = dot(vt[:, :seen], e_scr[i % 2, :seen, :]) * inverse
        atts[tile, :] = o_t.T.astype(bf16)
        do_t = (dos[tile, :].T.astype(f32) * inverse).astype(bf16)
        delta = jnp.sum(do_t.astype(f32) * o_t, axis=0, keepdims=True)
        kept[i] = do_t, delta

    def backward(i):
        tile = slice(i * TILE, (i + 1) * TILE)
        seen = (i + 1) * TILE
        do_t, delta = kept[i]
        do = do_t.T
        q = qs[tile, :]
        for c in range(i + 1):
            keys = slice(c * TILE, (c + 1) * TILE)
            e = e_scr[i % 2, keys, :]
            value_part = dot(e, do)
            dp = dot(vs[keys, :], do_t)
            ds = (e.astype(f32) * (dp - delta)).astype(bf16)
            ds_scr[i % 2, keys, :] = ds
            key_part = dot(ds, q)
            if c == i:
                dv[keys, :] = value_part
                dk[keys, :] = key_part
            else:
                dv[keys, :] += value_part
                dk[keys, :] += key_part
        gq = (dot(kt[:, :seen], ds_scr[i % 2, :seen, :]) * scale).T
        dqs[tile, :] = gq.astype(bf16)
        return weighted(gq, q, i * TILE)

    scores(0)
    for i in range(tiles):
        forward(i)
        if i + 1 < tiles:
            scores(i + 1)
        angle_sum = angle_sum + backward(i)

    for i in range(tiles):
        tile = slice(i * TILE, (i + 1) * TILE)
        gk = dk[tile, :] * scale
        dk[tile, :] = gk
        angle_sum = angle_sum + weighted(gk, ks[tile, :], i * TILE)

    for slot in range(2 * sources):
        at = pl.ds(pl.multiple_of(order_ref[slot] * half_rows, half_rows), half_rows)
        for number, ref in enumerate((atts, dqs, dk, dv)):
            start = number * rows + (slot % 2) * half_rows
            out_ref[slot // 2, start:start + half_rows, :] = ref[at, :].astype(bf16)
    line = jnp.sum(angle_sum, axis=0, keepdims=True)
    high = line.astype(bf16).astype(f32)
    middle = (line - high).astype(bf16).astype(f32)
    low = line - high - middle
    which = lax.broadcasted_iota(jnp.int32, (LOG_ROWS, HEAD), 0)
    packed = jnp.where(which == 0, high, jnp.where(which == 1, middle, jnp.where(which == 2, low, 0.0)))
    for source in range(sources):
        out_ref[source, 4 * rows:, :] = packed.astype(bf16)


def after_kernel(in_ref, cos_ref, sin_ref, att_ref, dq_ref, dk_ref, dv_ref):
    rows = cos_ref.shape[0]
    heads = in_ref.shape[0]
    group = att_ref.shape[1] // dk_ref.shape[1]
    cosine, signed = cos_ref[...], sin_ref[...]

    def back(u):
        return (u * cosine - swap_halves(u) * signed).astype(bf16)

    for kv in range(heads // group):
        key_sum = jnp.zeros((rows, HEAD), f32)
        value_sum = jnp.zeros((rows, HEAD), f32)
        for head in range(kv * group, (kv + 1) * group):
            cols = slice(head * HEAD, (head + 1) * HEAD)
            att_ref[:, cols] = in_ref[head, 0:rows]
            dq_ref[:, cols] = back(in_ref[head, rows:2 * rows].astype(f32))
            key_sum = key_sum + in_ref[head, 2 * rows:3 * rows].astype(f32)
            value_sum = value_sum + in_ref[head, 3 * rows:4 * rows].astype(f32)
        cols = slice(kv * HEAD, (kv + 1) * HEAD)
        dk_ref[:, cols] = back(key_sum)
        dv_ref[:, cols] = value_sum.astype(bf16)


def shape(*dims, dtype=bf16):
    return jax.ShapeDtypeStruct(dims, dtype)


def on_device(queries, key_rows, values, prior, later, order, table, index):
    rows, width = queries.shape[2:]
    kv_width = key_rows.shape[3]
    heads = width // HEAD
    sources = lax.axis_size("ctx")
    pipe = lax.axis_size("pipe")
    tokens = rows * sources
    arriving = lax.ppermute(prior, "pipe", [(i, (i + 1) % pipe) for i in range(pipe)])
    returning = lax.ppermute(later, "pipe", [(i, (i - 1) % pipe) for i in range(pipe)])
    params = pltpu.CompilerParams(vmem_limit_bytes=40 * 2**20)

    sent, cosine, sine = pl.pallas_call(
        before_kernel,
        out_shape=(shape(heads, 4 * rows, HEAD), shape(rows, HEAD, dtype=f32), shape(rows, HEAD, dtype=f32)),
        in_specs=[HBM] * 8,
        out_specs=[HBM] * 3,
        scratch_shapes=[
            pltpu.SMEM(order.shape, jnp.int32),
            pltpu.SMEM(table.shape, f32),
            pltpu.VMEM(index.shape, jnp.int32),
            pltpu.VMEM((rows, width), bf16),
            pltpu.VMEM((rows, kv_width), bf16),
            pltpu.VMEM((rows, width), bf16),
            pltpu.VMEM((rows, width), bf16),
            pltpu.VMEM((rows, kv_width), bf16),
            pltpu.VMEM((heads, rows, HEAD), bf16),
            pltpu.VMEM((kv_width // HEAD, rows, HEAD), bf16),
            pltpu.VMEM((rows, HEAD), f32),
            pltpu.VMEM((rows, HEAD), f32),
            pltpu.SemaphoreType.DMA((8,)),
        ]
        + [pltpu.SemaphoreType.DMA((heads,))] * 4
        + [pltpu.SemaphoreType.DMA((2,))],
        compiler_params=pltpu.CompilerParams(vmem_limit_bytes=56 * 2**20),
    )(order, table, index, queries[0, 0], key_rows[0, 0], values[0, 0], arriving[0, 0], returning[0, 0])

    held = lax.all_to_all(sent, "ctx", 0, 0)

    done = pl.pallas_call(
        main_kernel,
        out_shape=shape(sources, 4 * rows + LOG_ROWS, HEAD),
        in_specs=[SMEM, VMEM],
        out_specs=VMEM,
        scratch_shapes=[pltpu.VMEM((tokens, HEAD), bf16)] * 4
        + [pltpu.VMEM((HEAD, tokens), bf16)] * 2
        + [pltpu.VMEM((tokens, HEAD), f32)] * 2
        + [pltpu.VMEM((tokens, HEAD), bf16)] * 2
        + [pltpu.VMEM((2, tokens, TILE), f32)]
        + [pltpu.VMEM((2, tokens, TILE), bf16)] * 2,
        compiler_params=params,
    )(order, held)

    back = lax.all_to_all(done, "ctx", 0, 0)

    line = jnp.sum(back[:, 4 * rows:4 * rows + 3, :].astype(f32), axis=(0, 1))
    dp = lax.axis_size("dp")
    terms = [lax.ppermute(line, "dp", [(i, i ^ s) for i in range(dp)]) for s in range(1, dp)]

    attended, dq, dk, dv = pl.pallas_call(
        after_kernel,
        out_shape=(shape(rows, width), shape(rows, width), shape(rows, kv_width), shape(rows, kv_width)),
        in_specs=[VMEM] * 3,
        out_specs=[VMEM] * 4,
        compiler_params=params,
    )(back, cosine, sine)

    level = [line] + terms
    while len(level) > 1:
        level = [a + b for a, b in zip(level[0::2], level[1::2])]
    line = level[0]
    base = ROPE_BASE ** (-(jnp.arange(HALF, dtype=f32) * 2.0 / HEAD))
    onehot = (index[0][:, None] == jnp.arange(table.shape[1], dtype=jnp.int32)[None, :]).astype(f32)
    log_factor = jnp.sum(onehot * table[0][None, :], axis=1)
    log_gradient = (line[:HALF] - line[HALF:]) * base * jnp.exp(-log_factor)
    table_grad = jnp.sum(onehot * log_gradient[:, None], axis=0) / (tokens * dp)
    return attended[None, None], dq[None, None], dk[None, None], dv[None, None], table_grad[None, :]


def solution(mesh):
    block = P("pipe", "dp", "ctx", None)
    return jax.shard_map(
        on_device,
        mesh=mesh,
        in_specs=(block,) * 5 + (P(), P("pipe", None), P("pipe", None)),
        out_specs=(block,) * 4 + (P("pipe", None),),
        check_vma=False,
    )
```

```python
import math

import jax
import jax.numpy as jnp
from jax import lax
from jax.experimental import pallas as pl
from jax.experimental.pallas import tpu as pltpu
from jax.sharding import PartitionSpec as P

HEAD = 128
HALF = 64
ROPE_BASE = 500000.0
LOG_ROWS = 16
TILE = 512
RING = 4
LOG2E = math.log2(math.e)

VMEM = pl.BlockSpec(memory_space=pltpu.VMEM)
SMEM = pl.BlockSpec(memory_space=pltpu.SMEM)
ANY = pl.BlockSpec(memory_space=pl.ANY)
HBM = pl.BlockSpec(memory_space=pltpu.HBM)
f32 = jnp.float32
bf16 = jnp.bfloat16


def dot(a, b):
    return jnp.dot(a, b, preferred_element_type=f32)


def dot_nt(a, b):
    return lax.dot_general(a, b, (((1,), (1,)), ((), ())), preferred_element_type=f32)


def swap_halves(u):
    return pltpu.roll(u, HALF, 1)


def half_rates(table_ref, index_row):
    pair = lax.broadcasted_iota(jnp.int32, (1, HALF), 1).astype(f32)
    log_factor = jnp.zeros((1, HALF), f32)
    for entry in range(table_ref.shape[1]):
        log_factor = jnp.where(index_row == entry, table_ref[0, entry], log_factor)
    return jnp.exp(-pair * (2.0 / HEAD * math.log(ROPE_BASE)) - log_factor)


def before_kernel(order_hbm, table_hbm, index_hbm, q_hbm, k_hbm, v_hbm, prior_hbm, do_hbm,
                  out_hbm, cos_hbm, sin_hbm,
                  order_ref, table_ref, index_ref, q_ref, k_ref, prior_ref, do_ref, v_ref, packed_q, packed_k, cos_ref, sin_ref,
                  in_sems, do_sems, v_sems, q_sems, k_sems, wave_sems):
    rows, width = q_ref.shape
    half_rows = rows // 2
    heads = width // HEAD
    group = width // k_ref.shape[1]
    pairs = ((order_hbm, order_ref), (table_hbm, table_ref), (index_hbm, index_ref),
             (k_hbm, k_ref), (q_hbm, q_ref), (prior_hbm, prior_ref), (do_hbm, do_ref), (v_hbm, v_ref))
    copies = [pltpu.make_async_copy(a, b, in_sems.at[i]) for i, (a, b) in enumerate(pairs)]
    for copy in copies:
        copy.start()
    sent = []

    def send(source, kv, part, sem):
        copy = pltpu.make_async_copy(source, out_hbm.at[kv, pl.ds(part * rows, rows), :], sem)
        copy.start()
        sent.append(copy)

    for copy in copies[:3]:
        copy.wait()
    me = lax.axis_index("ctx")
    rate = half_rates(table_ref, index_ref[...])
    row = lax.broadcasted_iota(jnp.int32, (rows, HALF), 0)
    first, second = order_ref[2 * me] * half_rows, order_ref[2 * me + 1] * half_rows
    position = jnp.where(row < half_rows, first + row, second + row - half_rows).astype(f32)
    angle = position * rate
    cosine = jnp.cos(angle)
    sine = jnp.sin(angle)
    cosine = jnp.concatenate([cosine, cosine], axis=1)
    signed = jnp.concatenate([-sine, sine], axis=1)
    cos_ref[...] = cosine
    sin_ref[...] = signed
    for number, (a, b) in enumerate(((cos_ref, cos_hbm), (sin_ref, sin_hbm))):
        copy = pltpu.make_async_copy(a, b, wave_sems.at[number])
        copy.start()
        sent.append(copy)
    copies[6].wait()
    copies[7].wait()
    for head in range(heads):
        send(do_ref.at[:, pl.ds(head * HEAD, HEAD)], head // group, group + head % group, do_sems.at[head])
    for kv in range(heads // group):
        send(v_ref.at[:, pl.ds(kv * HEAD, HEAD)], kv, 2 * group + 1, v_sems.at[kv])
    copies[3].wait()
    for kv in range(heads // group):
        u = k_ref[:, kv * HEAD:(kv + 1) * HEAD].astype(f32)
        packed_k[kv] = (u * cosine + swap_halves(u) * signed).astype(bf16)
        send(packed_k.at[kv], kv, 2 * group, k_sems.at[kv])
    copies[4].wait()
    copies[5].wait()
    for head in range(heads):
        cols = slice(head * HEAD, (head + 1) * HEAD)
        u = q_ref[:, cols].astype(f32) + prior_ref[:, cols].astype(f32)
        packed_q[head] = (u * cosine + swap_halves(u) * signed).astype(bf16)
        send(packed_q.at[head], head // group, head % group, q_sems.at[head])
    for copy in sent:
        copy.wait()


def placed_at():
    chip = lax.axis_index("ctx")
    core = lax.axis_index("pipe")
    row, column = chip // RING, chip % RING
    return core == 0, jnp.where(core == 0, row, column), jnp.where(core == 0, column, row)


def main_kernel(order_ref, in_ref, own_ref, next_ref, far_ref, last_ref,
                out_ref, grad_own, grad_next, grad_far, grad_last,
                qs, dos, ks, vs, kt, vt, dk, dv, atts, dqs, s_scr, e_scr, ds_scr, angle_ref, place_ref):
    rows = own_ref.shape[1] // 2
    half_rows = rows // 2
    group = in_ref.shape[1] // rows // 2 - 1
    tokens = ks.shape[0]
    block = group * half_rows
    scale = HEAD ** -0.5
    coef = scale * LOG2E
    straight, _, column = placed_at()

    def slot_of(rank, offset, half):
        at = lax.rem(column + offset, RING)
        return order_ref[2 * jnp.where(straight, rank * RING + at, at * RING + rank) + half]

    def half_block(ref, number):
        return ref.at[pl.ds(pl.multiple_of(number * half_rows, half_rows), half_rows), :]

    pieces = [(rank, half) for rank in range(RING) for half in range(2)]
    keys_of = [own_ref, next_ref, far_ref, last_ref]
    for offset, ref in enumerate(keys_of):
        for rank, half in pieces:
            number = slot_of(rank, offset, half)
            half_block(ks, number)[...] = ref[rank, half * half_rows:(half + 1) * half_rows, :]
            half_block(vs, number)[...] = ref[rank, rows + half * half_rows:rows + (half + 1) * half_rows, :]
    places = [slot_of(rank, 0, half) for rank, half in pieces]
    ranks = []
    for place in places:
        above = jnp.int32(0)
        for other in places:
            above = above + jnp.where(other < place, 1, 0)
        ranks.append(above)
        place_ref[above] = place
    for (rank, half), at in zip(pieces, ranks):
        for head in range(group):
            start = head * rows + half * half_rows
            half_block(qs, at * group + head)[...] = in_ref[rank, start:start + half_rows, :]
            start = start + group * rows
            half_block(dos, at * group + head)[...] = in_ref[rank, start:start + half_rows, :]
    kt[...] = ks[...].T
    vt[...] = vs[...].T
    dk[...] = jnp.zeros_like(dk)
    dv[...] = jnp.zeros_like(dv)
    angle_ref[...] = jnp.zeros_like(angle_ref)

    key_iota = lax.broadcasted_iota(jnp.int32, (TILE, TILE), 0)
    lane = lax.broadcasted_iota(jnp.int32, (1, TILE), 1)
    line = lax.broadcasted_iota(jnp.int32, (TILE, 1), 0)
    row_number = lax.broadcasted_iota(jnp.int32, (TILE, HEAD), 0)

    def weighted(gradient, rotated, position):
        term = gradient * swap_halves(rotated.astype(f32)) * position
        return jnp.sum(term.reshape(TILE // 8, 8, HEAD), axis=0)

    def attend(m, chunks):
        low, high = place_ref[2 * m] * half_rows, place_ref[2 * m + 1] * half_rows
        tile = pl.ds(pl.multiple_of(m * TILE, TILE), TILE)
        seen = chunks * TILE
        q = qs[tile, :]
        position = jnp.where(lane < block, low, high) + lax.rem(lane, half_rows)
        top = None
        for c in range(chunks):
            keys = slice(c * TILE, (c + 1) * TILE)
            s = dot_nt(ks[keys, :], q)
            s = jnp.where(key_iota <= position - c * TILE, s, -1e30)
            s_scr[keys, :] = s
            peak = jnp.max(s, axis=0, keepdims=True)
            top = peak if top is None else jnp.maximum(top, peak)
        top = top * coef
        total = jnp.zeros((1, TILE), f32)
        for c in range(chunks):
            keys = slice(c * TILE, (c + 1) * TILE)
            e = jnp.exp2(s_scr[keys, :] * coef - top)
            total = total + jnp.sum(e, axis=0, keepdims=True)
            e_scr[keys, :] = e.astype(bf16)
        inverse = 1.0 / total
        o_t = dot(vt[:, :seen], e_scr[:seen, :]) * inverse
        atts[tile, :] = o_t.T.astype(bf16)
        do_t = (dos[tile, :].T.astype(f32) * inverse).astype(bf16)
        delta = jnp.sum(do_t.astype(f32) * o_t, axis=0, keepdims=True)
        do = do_t.T
        for c in range(chunks):
            keys = slice(c * TILE, (c + 1) * TILE)
            e = e_scr[keys, :]
            dv[keys, :] += dot(e, do)
            dp = dot(vs[keys, :], do_t)
            ds = (e.astype(f32) * (dp - delta)).astype(bf16)
            ds_scr[keys, :] = ds
            dk[keys, :] += dot(ds, q)
        gq = (dot(kt[:, :seen], ds_scr[:seen, :]) * scale).T
        dqs[tile, :] = gq.astype(bf16)
        at = (jnp.where(line < block, low, high) + lax.rem(line, half_rows)).astype(f32)
        angle_ref[...] += weighted(gq, q, at)

    def one_tile(m, carry):
        chunks = place_ref[2 * m + 1] * half_rows // TILE
        for n in range(tokens // TILE):
            @pl.when(chunks == n)
            def _():
                attend(m, n + 1)
        return carry

    lax.fori_loop(0, qs.shape[0] // TILE, one_tile, 0)

    for i in range(tokens // TILE):
        tile = slice(i * TILE, (i + 1) * TILE)
        gk = dk[tile, :] * scale
        dk[tile, :] = gk
        angle_ref[...] += weighted(gk, ks[tile, :], (row_number + i * TILE).astype(f32))

    for (rank, half), at in zip(pieces, ranks):
        for head in range(group):
            start = head * rows + half * half_rows
            out_ref[rank, start:start + half_rows, :] = half_block(atts, at * group + head)[...]
            start = start + group * rows
            out_ref[rank, start:start + half_rows, :] = half_block(dqs, at * group + head)[...]
    packed = split_line(jnp.sum(angle_ref[...], axis=0, keepdims=True))
    for offset, ref in enumerate((grad_own, grad_next, grad_far, grad_last)):
        for rank, half in pieces:
            number = slot_of(rank, offset, half)
            start = half * half_rows
            ref[rank, start:start + half_rows, :] = half_block(dk, number)[...].astype(bf16)
            ref[rank, rows + start:rows + start + half_rows, :] = half_block(dv, number)[...].astype(bf16)
        for rank in range(RING):
            ref[rank, 2 * rows:, :] = packed


def split_line(line):
    high = line.astype(bf16).astype(f32)
    middle = (line - high).astype(bf16).astype(f32)
    low = line - high - middle
    which = lax.broadcasted_iota(jnp.int32, (LOG_ROWS, HEAD), 0)
    packed = jnp.where(which == 0, high, jnp.where(which == 1, middle, jnp.where(which == 2, low, 0.0)))
    return packed.astype(bf16)


def sum_kernel(held_ref, own_ref, next_ref, far_ref, last_ref, out_ref):
    grads = (own_ref, next_ref, far_ref, last_ref)
    size = own_ref.shape[1] - LOG_ROWS
    start = out_ref.shape[1] - LOG_ROWS - size
    for rank in range(RING):
        total = grads[0][rank, :size].astype(f32)
        for ref in grads[1:]:
            total = total + ref[rank, :size].astype(f32)
        out_ref[rank, start:start + size, :] = total.astype(bf16)
    _, _, column = placed_at()
    lines = [jnp.sum(ref[0, size:].astype(f32), axis=0, keepdims=True) for ref in grads]
    line = jnp.zeros((1, HEAD), f32)
    for at in range(RING):
        offset = lax.rem(column - at + RING, RING)
        term = lines[0]
        for number in range(1, RING):
            term = jnp.where(offset == number, lines[number], term)
        line = line + term
    packed = split_line(line)
    for rank in range(RING):
        out_ref[rank, start + size:, :] = packed


def after_kernel(in_ref, cos_ref, sin_ref, att_ref, dq_ref, dk_ref, dv_ref):
    rows = cos_ref.shape[0]
    group = att_ref.shape[1] // dk_ref.shape[1]
    cosine, signed = cos_ref[...], sin_ref[...]

    def back(u):
        u = u.astype(f32)
        return (u * cosine - swap_halves(u) * signed).astype(bf16)

    for kv in range(RING):
        for number in range(group):
            head = kv * group + number
            cols = slice(head * HEAD, (head + 1) * HEAD)
            att_ref[:, cols] = in_ref[kv, number * rows:(number + 1) * rows]
            dq_ref[:, cols] = back(in_ref[kv, (group + number) * rows:(group + number + 1) * rows])
        cols = slice(kv * HEAD, (kv + 1) * HEAD)
        start = 2 * group * rows
        dk_ref[:, cols] = back(in_ref[kv, start:start + rows])
        dv_ref[:, cols] = in_ref[kv, start + rows:start + 2 * rows]


def shape(*dims, dtype=bf16):
    return jax.ShapeDtypeStruct(dims, dtype)


def on_device(queries, key_rows, values, prior, later, order, table, index):
    rows, width = queries.shape[2:]
    kv_width = key_rows.shape[3]
    heads = width // HEAD
    sources = lax.axis_size("ctx")
    pipe = lax.axis_size("pipe")
    tokens = rows * sources
    group = width // kv_width
    arriving = lax.ppermute(prior, "pipe", [(i, (i + 1) % pipe) for i in range(pipe)])
    returning = lax.ppermute(later, "pipe", [(i, (i - 1) % pipe) for i in range(pipe)])
    params = pltpu.CompilerParams(vmem_limit_bytes=40 * 2**20)
    both = ("pipe", "ctx")

    def device(core, rank, column):
        return core * sources + (rank * RING + column if core == 0 else column * RING + rank)

    heads_over = [[device(core, rank, column) for rank in range(RING)]
                  for core in range(pipe) for column in range(RING)]

    def moved(value, by):
        pairs = [(device(core, rank, column), device(core, rank, (column + by) % RING))
                 for core in range(pipe) for rank in range(RING) for column in range(RING)]
        return lax.ppermute(value, both, pairs)

    sent, cosine, sine = pl.pallas_call(
        before_kernel,
        out_shape=(shape(RING, 2 * (group + 1) * rows, HEAD), shape(rows, HEAD, dtype=f32), shape(rows, HEAD, dtype=f32)),
        in_specs=[HBM] * 8,
        out_specs=[HBM] * 3,
        scratch_shapes=[
            pltpu.SMEM(order.shape, jnp.int32),
            pltpu.SMEM(table.shape, f32),
            pltpu.VMEM(index.shape, jnp.int32),
            pltpu.VMEM((rows, width), bf16),
            pltpu.VMEM((rows, kv_width), bf16),
            pltpu.VMEM((rows, width), bf16),
            pltpu.VMEM((rows, width), bf16),
            pltpu.VMEM((rows, kv_width), bf16),
            pltpu.VMEM((heads, rows, HEAD), bf16),
            pltpu.VMEM((kv_width // HEAD, rows, HEAD), bf16),
            pltpu.VMEM((rows, HEAD), f32),
            pltpu.VMEM((rows, HEAD), f32),
            pltpu.SemaphoreType.DMA((8,)),
        ]
        + [pltpu.SemaphoreType.DMA((heads,))] * 4
        + [pltpu.SemaphoreType.DMA((2,))],
        compiler_params=pltpu.CompilerParams(vmem_limit_bytes=56 * 2**20),
    )(order, table, index, queries[0, 0], key_rows[0, 0], values[0, 0], arriving[0, 0], returning[0, 0])

    held = lax.all_to_all(sent, both, 0, 0, axis_index_groups=heads_over)
    own = held[:, 2 * group * rows:, :]
    others = [moved(own, RING - offset) for offset in range(1, RING)]

    grads = shape(RING, 2 * rows + LOG_ROWS, HEAD)
    done, *grads = pl.pallas_call(
        main_kernel,
        out_shape=[shape(RING, 2 * (group + 1) * rows + LOG_ROWS, HEAD)] + [grads] * RING,
        in_specs=[SMEM] + [VMEM] * (1 + RING),
        out_specs=[VMEM] * (1 + RING),
        scratch_shapes=[pltpu.VMEM((tokens, HEAD), bf16)] * 4
        + [pltpu.VMEM((HEAD, tokens), bf16)] * 2
        + [pltpu.VMEM((tokens, HEAD), f32)] * 2
        + [pltpu.VMEM((tokens, HEAD), bf16)] * 2
        + [pltpu.VMEM((tokens, TILE), f32)]
        + [pltpu.VMEM((tokens, TILE), bf16)] * 2
        + [pltpu.VMEM((8, HEAD), f32), pltpu.SMEM((2 * RING,), jnp.int32)],
        compiler_params=params,
    )(order, held, own, *others)
    arrived = [moved(grads[offset], offset) for offset in range(1, RING)]
    done = pl.pallas_call(
        sum_kernel,
        out_shape=shape(*done.shape),
        in_specs=[ANY] + [VMEM] * RING,
        out_specs=VMEM,
        input_output_aliases={0: 0},
        compiler_params=params,
    )(done, grads[0], *arrived)
    back = lax.all_to_all(done, both, 0, 0, axis_index_groups=heads_over)

    line = jnp.sum(back[:, -LOG_ROWS:-LOG_ROWS + 3, :].astype(f32), axis=(0, 1))
    dp = lax.axis_size("dp")
    terms = [lax.ppermute(line, "dp", [(i, i ^ s) for i in range(dp)]) for s in range(1, dp)]

    attended, dq, dk, dv = pl.pallas_call(
        after_kernel,
        out_shape=(shape(rows, width), shape(rows, width), shape(rows, kv_width), shape(rows, kv_width)),
        in_specs=[VMEM] * 3,
        out_specs=[VMEM] * 4,
        compiler_params=params,
    )(back, cosine, sine)

    level = [line] + terms
    while len(level) > 1:
        level = [a + b for a, b in zip(level[0::2], level[1::2])]
    line = level[0]
    base = ROPE_BASE ** (-(jnp.arange(HALF, dtype=f32) * 2.0 / HEAD))
    onehot = (index[0][:, None] == jnp.arange(table.shape[1], dtype=jnp.int32)[None, :]).astype(f32)
    log_factor = jnp.sum(onehot * table[0][None, :], axis=1)
    log_gradient = (line[:HALF] - line[HALF:]) * base * jnp.exp(-log_factor)
    table_grad = jnp.sum(onehot * log_gradient[:, None], axis=0) / (tokens * dp)
    return attended[None, None], dq[None, None], dk[None, None], dv[None, None], table_grad[None, :]


def solution(mesh):
    block = P("pipe", "dp", "ctx", None)
    return jax.shard_map(
        on_device,
        mesh=mesh,
        in_specs=(block,) * 5 + (P(), P("pipe", None), P("pipe", None)),
        out_specs=(block,) * 4 + (P("pipe", None),),
        check_vma=False,
    )
```

```python
import math

import jax
import jax.numpy as jnp
from jax import lax
from jax.experimental import pallas as pl
from jax.experimental.pallas import tpu as pltpu
from jax.sharding import PartitionSpec as P

HEAD = 128
HALF = 64
ROPE_BASE = 500000.0
LOG_ROWS = 16
TILE = 512
RING = 4
LOG2E = math.log2(math.e)

VMEM = pl.BlockSpec(memory_space=pltpu.VMEM)
SMEM = pl.BlockSpec(memory_space=pltpu.SMEM)
ANY = pl.BlockSpec(memory_space=pl.ANY)
HBM = pl.BlockSpec(memory_space=pltpu.HBM)
f32 = jnp.float32
bf16 = jnp.bfloat16


def dot(a, b):
    return jnp.dot(a, b, preferred_element_type=f32)


def dot_nt(a, b):
    return lax.dot_general(a, b, (((1,), (1,)), ((), ())), preferred_element_type=f32)


def swap_halves(u):
    return pltpu.roll(u, HALF, 1)


def half_rates(table_ref, index_row):
    pair = lax.broadcasted_iota(jnp.int32, (1, HALF), 1).astype(f32)
    log_factor = jnp.zeros((1, HALF), f32)
    for entry in range(table_ref.shape[1]):
        log_factor = jnp.where(index_row == entry, table_ref[0, entry], log_factor)
    return jnp.exp(-pair * (2.0 / HEAD * math.log(ROPE_BASE)) - log_factor)


def first_kernel(order_hbm, table_hbm, index_hbm, k_hbm, v_hbm,
                 out_hbm, cos_hbm, sin_hbm,
                 order_ref, table_ref, index_ref, k_ref, v_ref, packed_k, cos_ref, sin_ref,
                 in_sems, v_sems, k_sems, wave_sems):
    rows = k_ref.shape[0]
    half_rows = rows // 2
    kv_heads = k_ref.shape[1] // HEAD
    start = out_hbm.shape[1] - 2 * rows
    pairs = ((order_hbm, order_ref), (table_hbm, table_ref), (index_hbm, index_ref), (k_hbm, k_ref), (v_hbm, v_ref))
    copies = [pltpu.make_async_copy(a, b, in_sems.at[i]) for i, (a, b) in enumerate(pairs)]
    for copy in copies:
        copy.start()
    sent = []

    def send(source, to, sem):
        copy = pltpu.make_async_copy(source, to, sem)
        copy.start()
        sent.append(copy)

    for copy in copies[:3]:
        copy.wait()
    me = lax.axis_index("ctx")
    rate = half_rates(table_ref, index_ref[...])
    row = lax.broadcasted_iota(jnp.int32, (rows, HALF), 0)
    first, second = order_ref[2 * me] * half_rows, order_ref[2 * me + 1] * half_rows
    position = jnp.where(row < half_rows, first + row, second + row - half_rows).astype(f32)
    angle = position * rate
    cosine = jnp.cos(angle)
    sine = jnp.sin(angle)
    cosine = jnp.concatenate([cosine, cosine], axis=1)
    signed = jnp.concatenate([-sine, sine], axis=1)
    cos_ref[...] = cosine
    sin_ref[...] = signed
    send(cos_ref, cos_hbm, wave_sems.at[0])
    send(sin_ref, sin_hbm, wave_sems.at[1])
    copies[3].wait()
    copies[4].wait()
    for kv in range(kv_heads):
        cols = slice(kv * HEAD, (kv + 1) * HEAD)
        send(v_ref.at[:, pl.ds(kv * HEAD, HEAD)], out_hbm.at[kv, pl.ds(start + rows, rows), :], v_sems.at[kv])
        u = k_ref[:, cols].astype(f32)
        packed_k[kv] = (u * cosine + swap_halves(u) * signed).astype(bf16)
        send(packed_k.at[kv], out_hbm.at[kv, pl.ds(start, rows), :], k_sems.at[kv])
    for copy in sent:
        copy.wait()


def second_kernel(held_hbm, cos_hbm, sin_hbm, q_hbm, prior_hbm, do_hbm, out_hbm,
                  cos_ref, sin_ref, q_ref, prior_ref, do_ref, packed_q, in_sems, do_sems, q_sems):
    rows, width = q_ref.shape
    heads = width // HEAD
    group = heads // out_hbm.shape[0]
    copies = [pltpu.make_async_copy(cos_hbm, cos_ref, in_sems.at[0]), pltpu.make_async_copy(sin_hbm, sin_ref, in_sems.at[1])]
    for kv in range(heads // group):
        cols = pl.ds(kv * group * HEAD, group * HEAD)
        for a, b in ((q_hbm, q_ref), (prior_hbm, prior_ref), (do_hbm, do_ref)):
            copies.append(pltpu.make_async_copy(a.at[:, cols], b.at[:, cols], in_sems.at[len(copies)]))
    for copy in copies:
        copy.start()
    sent = []

    def send(source, head, part, sem):
        to = out_hbm.at[head // group, pl.ds((part * group + head % group) * rows, rows), :]
        copy = pltpu.make_async_copy(source, to, sem)
        copy.start()
        sent.append(copy)

    for copy in copies[:2]:
        copy.wait()
    cosine, signed = cos_ref[...], sin_ref[...]
    for head in range(heads):
        cols = slice(head * HEAD, (head + 1) * HEAD)
        if head % group == 0:
            for copy in copies[2 + 3 * (head // group):5 + 3 * (head // group)]:
                copy.wait()
        u = q_ref[:, cols].astype(f32) + prior_ref[:, cols].astype(f32)
        packed_q[head] = (u * cosine + swap_halves(u) * signed).astype(bf16)
        send(packed_q.at[head], head, 0, q_sems.at[head])
        send(do_ref.at[:, pl.ds(head * HEAD, HEAD)], head, 1, do_sems.at[head])
    for copy in sent:
        copy.wait()


def placed_at():
    chip = lax.axis_index("ctx")
    core = lax.axis_index("pipe")
    row, column = chip // RING, chip % RING
    return core == 0, jnp.where(core == 0, row, column), jnp.where(core == 0, column, row)


def main_kernel(order_ref, in_ref, own_ref, next_ref, far_ref, last_ref,
                out_ref, grad_own, grad_next, grad_far, grad_last,
                qs, dos, ks, vs, kt, vt, dk, dv, atts, dqs, s_scr, e_scr, ds_scr, angle_ref, place_ref):
    rows = own_ref.shape[1] // 2
    half_rows = rows // 2
    group = in_ref.shape[1] // rows // 2 - 1
    tokens = ks.shape[0]
    block = group * half_rows
    scale = HEAD ** -0.5
    coef = scale * LOG2E
    straight, _, column = placed_at()

    def slot_of(rank, offset, half):
        at = lax.rem(column + offset, RING)
        return order_ref[2 * jnp.where(straight, rank * RING + at, at * RING + rank) + half]

    def half_block(ref, number):
        return ref.at[pl.ds(pl.multiple_of(number * half_rows, half_rows), half_rows), :]

    pieces = [(rank, half) for rank in range(RING) for half in range(2)]
    keys_of = [own_ref, next_ref, far_ref, last_ref]
    for offset, ref in enumerate(keys_of):
        for rank, half in pieces:
            number = slot_of(rank, offset, half)
            half_block(ks, number)[...] = ref[rank, half * half_rows:(half + 1) * half_rows, :]
            half_block(vs, number)[...] = ref[rank, rows + half * half_rows:rows + (half + 1) * half_rows, :]
    places = [slot_of(rank, 0, half) for rank, half in pieces]
    ranks = []
    for place in places:
        above = jnp.int32(0)
        for other in places:
            above = above + jnp.where(other < place, 1, 0)
        ranks.append(above)
        place_ref[above] = place
    for (rank, half), at in zip(pieces, ranks):
        for head in range(group):
            start = head * rows + half * half_rows
            half_block(qs, at * group + head)[...] = in_ref[rank, start:start + half_rows, :]
            start = start + group * rows
            half_block(dos, at * group + head)[...] = in_ref[rank, start:start + half_rows, :]
    kt[...] = ks[...].T
    vt[...] = vs[...].T
    dk[...] = jnp.zeros_like(dk)
    dv[...] = jnp.zeros_like(dv)
    angle_ref[...] = jnp.zeros_like(angle_ref)

    key_iota = lax.broadcasted_iota(jnp.int32, (TILE, TILE), 0)
    lane = lax.broadcasted_iota(jnp.int32, (1, TILE), 1)
    line = lax.broadcasted_iota(jnp.int32, (TILE, 1), 0)
    row_number = lax.broadcasted_iota(jnp.int32, (TILE, HEAD), 0)

    def weighted(gradient, rotated, position):
        term = gradient * swap_halves(rotated.astype(f32)) * position
        return jnp.sum(term.reshape(TILE // 8, 8, HEAD), axis=0)

    def attend(m, chunks):
        low, high = place_ref[2 * m] * half_rows, place_ref[2 * m + 1] * half_rows
        tile = pl.ds(pl.multiple_of(m * TILE, TILE), TILE)
        seen = chunks * TILE
        q = qs[tile, :]
        position = jnp.where(lane < block, low, high) + lax.rem(lane, half_rows)
        top = None
        for c in range(chunks):
            keys = slice(c * TILE, (c + 1) * TILE)
            s = dot_nt(ks[keys, :], q)
            s = jnp.where(key_iota <= position - c * TILE, s, -1e30)
            s_scr[keys, :] = s
            peak = jnp.max(s, axis=0, keepdims=True)
            top = peak if top is None else jnp.maximum(top, peak)
        top = top * coef
        total = jnp.zeros((1, TILE), f32)
        for c in range(chunks):
            keys = slice(c * TILE, (c + 1) * TILE)
            e = jnp.exp2(s_scr[keys, :] * coef - top)
            total = total + jnp.sum(e, axis=0, keepdims=True)
            e_scr[keys, :] = e.astype(bf16)
        inverse = 1.0 / total
        o_t = dot(vt[:, :seen], e_scr[:seen, :]) * inverse
        atts[tile, :] = o_t.T.astype(bf16)
        do_t = (dos[tile, :].T.astype(f32) * inverse).astype(bf16)
        delta = jnp.sum(do_t.astype(f32) * o_t, axis=0, keepdims=True)
        do = do_t.T
        for c in range(chunks):
            keys = slice(c * TILE, (c + 1) * TILE)
            e = e_scr[keys, :]
            dv[keys, :] += dot(e, do)
            dp = dot(vs[keys, :], do_t)
            ds = (e.astype(f32) * (dp - delta)).astype(bf16)
            ds_scr[keys, :] = ds
            dk[keys, :] += dot(ds, q)
        gq = (dot(kt[:, :seen], ds_scr[:seen, :]) * scale).T
        dqs[tile, :] = gq.astype(bf16)
        at = (jnp.where(line < block, low, high) + lax.rem(line, half_rows)).astype(f32)
        angle_ref[...] += weighted(gq, q, at)

    def one_tile(m, carry):
        chunks = place_ref[2 * m + 1] * half_rows // TILE
        for n in range(tokens // TILE):
            @pl.when(chunks == n)
            def _():
                attend(m, n + 1)
        return carry

    lax.fori_loop(0, qs.shape[0] // TILE, one_tile, 0)

    for i in range(tokens // TILE):
        tile = slice(i * TILE, (i + 1) * TILE)
        gk = dk[tile, :] * scale
        dk[tile, :] = gk
        angle_ref[...] += weighted(gk, ks[tile, :], (row_number + i * TILE).astype(f32))

    for (rank, half), at in zip(pieces, ranks):
        for head in range(group):
            start = head * rows + half * half_rows
            out_ref[rank, start:start + half_rows, :] = half_block(atts, at * group + head)[...]
            start = start + group * rows
            out_ref[rank, start:start + half_rows, :] = half_block(dqs, at * group + head)[...]
    packed = split_line(jnp.sum(angle_ref[...], axis=0, keepdims=True))
    for offset, ref in enumerate((grad_own, grad_next, grad_far, grad_last)):
        for rank, half in pieces:
            number = slot_of(rank, offset, half)
            start = half * half_rows
            ref[rank, start:start + half_rows, :] = half_block(dk, number)[...].astype(bf16)
            ref[rank, rows + start:rows + start + half_rows, :] = half_block(dv, number)[...].astype(bf16)
        for rank in range(RING):
            ref[rank, 2 * rows:, :] = packed


def split_line(line):
    high = line.astype(bf16).astype(f32)
    middle = (line - high).astype(bf16).astype(f32)
    low = line - high - middle
    which = lax.broadcasted_iota(jnp.int32, (LOG_ROWS, HEAD), 0)
    packed = jnp.where(which == 0, high, jnp.where(which == 1, middle, jnp.where(which == 2, low, 0.0)))
    return packed.astype(bf16)


def sum_kernel(held_ref, own_ref, next_ref, far_ref, last_ref, out_ref):
    grads = (own_ref, next_ref, far_ref, last_ref)
    size = own_ref.shape[1] - LOG_ROWS
    start = out_ref.shape[1] - LOG_ROWS - size
    for rank in range(RING):
        total = grads[0][rank, :size].astype(f32)
        for ref in grads[1:]:
            total = total + ref[rank, :size].astype(f32)
        out_ref[rank, start:start + size, :] = total.astype(bf16)
    _, _, column = placed_at()
    lines = [jnp.sum(ref[0, size:].astype(f32), axis=0, keepdims=True) for ref in grads]
    line = jnp.zeros((1, HEAD), f32)
    for at in range(RING):
        offset = lax.rem(column - at + RING, RING)
        term = lines[0]
        for number in range(1, RING):
            term = jnp.where(offset == number, lines[number], term)
        line = line + term
    packed = split_line(line)
    for rank in range(RING):
        out_ref[rank, start + size:, :] = packed


def after_kernel(in_ref, cos_ref, sin_ref, att_ref, dq_ref, dk_ref, dv_ref):
    rows = cos_ref.shape[0]
    group = att_ref.shape[1] // dk_ref.shape[1]
    cosine, signed = cos_ref[...], sin_ref[...]

    def back(u):
        u = u.astype(f32)
        return (u * cosine - swap_halves(u) * signed).astype(bf16)

    for kv in range(RING):
        for number in range(group):
            head = kv * group + number
            cols = slice(head * HEAD, (head + 1) * HEAD)
            att_ref[:, cols] = in_ref[kv, number * rows:(number + 1) * rows]
            dq_ref[:, cols] = back(in_ref[kv, (group + number) * rows:(group + number + 1) * rows])
        cols = slice(kv * HEAD, (kv + 1) * HEAD)
        start = 2 * group * rows
        dk_ref[:, cols] = back(in_ref[kv, start:start + rows])
        dv_ref[:, cols] = in_ref[kv, start + rows:start + 2 * rows]


def shape(*dims, dtype=bf16):
    return jax.ShapeDtypeStruct(dims, dtype)


def on_device(queries, key_rows, values, prior, later, order, table, index):
    rows, width = queries.shape[2:]
    kv_width = key_rows.shape[3]
    heads = width // HEAD
    sources = lax.axis_size("ctx")
    pipe = lax.axis_size("pipe")
    tokens = rows * sources
    group = width // kv_width
    arriving = lax.ppermute(prior, "pipe", [(i, (i + 1) % pipe) for i in range(pipe)])
    returning = lax.ppermute(later, "pipe", [(i, (i - 1) % pipe) for i in range(pipe)])
    params = pltpu.CompilerParams(vmem_limit_bytes=40 * 2**20)
    both = ("pipe", "ctx")

    def device(core, rank, column):
        return core * sources + (rank * RING + column if core == 0 else column * RING + rank)

    heads_over = [[device(core, rank, column) for rank in range(RING)]
                  for core in range(pipe) for column in range(RING)]

    def moved(value, by):
        pairs = [(device(core, rank, column), device(core, rank, (column + by) % RING))
                 for core in range(pipe) for rank in range(RING) for column in range(RING)]
        return lax.ppermute(value, both, pairs)

    payload = shape(RING, 2 * (group + 1) * rows, HEAD)
    wave = shape(rows, HEAD, dtype=f32)
    wide = pltpu.CompilerParams(vmem_limit_bytes=56 * 2**20)
    wave_buffer = pltpu.VMEM((rows, HEAD), f32)
    kv_buffer = pltpu.VMEM((rows, kv_width), bf16)
    buffer = pltpu.VMEM((rows, width), bf16)
    sent, cosine, sine = pl.pallas_call(
        first_kernel,
        out_shape=(payload, wave, wave),
        in_specs=[HBM] * 5,
        out_specs=[HBM] * 3,
        scratch_shapes=[
            pltpu.SMEM(order.shape, jnp.int32),
            pltpu.SMEM(table.shape, f32),
            pltpu.VMEM(index.shape, jnp.int32),
            kv_buffer,
            kv_buffer,
            pltpu.VMEM((RING, rows, HEAD), bf16),
            wave_buffer,
            wave_buffer,
            pltpu.SemaphoreType.DMA((5,)),
            pltpu.SemaphoreType.DMA((RING,)),
            pltpu.SemaphoreType.DMA((RING,)),
            pltpu.SemaphoreType.DMA((2,)),
        ],
        compiler_params=wide,
        cost_estimate=pl.CostEstimate(flops=10**7, bytes_accessed=4 * 10**6, transcendentals=0),
    )(order, table, index, key_rows[0, 0], values[0, 0])
    sent = pl.pallas_call(
        second_kernel,
        out_shape=payload,
        in_specs=[HBM] * 6,
        out_specs=HBM,
        scratch_shapes=[wave_buffer, wave_buffer, buffer, buffer, buffer, pltpu.VMEM((heads, rows, HEAD), bf16)]
        + [pltpu.SemaphoreType.DMA((2 + 3 * RING,))] + [pltpu.SemaphoreType.DMA((heads,))] * 2,
        input_output_aliases={0: 0},
        compiler_params=wide,
    )(sent, cosine, sine, queries[0, 0], arriving[0, 0], returning[0, 0])

    held = lax.all_to_all(sent, both, 0, 0, axis_index_groups=heads_over)
    own = held[:, 2 * group * rows:, :]
    others = [moved(own, RING - offset) for offset in range(1, RING)]

    grads = shape(RING, 2 * rows + LOG_ROWS, HEAD)
    done, *grads = pl.pallas_call(
        main_kernel,
        out_shape=[shape(RING, 2 * (group + 1) * rows + LOG_ROWS, HEAD)] + [grads] * RING,
        in_specs=[SMEM] + [VMEM] * (1 + RING),
        out_specs=[VMEM] * (1 + RING),
        scratch_shapes=[pltpu.VMEM((tokens, HEAD), bf16)] * 4
        + [pltpu.VMEM((HEAD, tokens), bf16)] * 2
        + [pltpu.VMEM((tokens, HEAD), f32)] * 2
        + [pltpu.VMEM((tokens, HEAD), bf16)] * 2
        + [pltpu.VMEM((tokens, TILE), f32)]
        + [pltpu.VMEM((tokens, TILE), bf16)] * 2
        + [pltpu.VMEM((8, HEAD), f32), pltpu.SMEM((2 * RING,), jnp.int32)],
        compiler_params=params,
    )(order, held, own, *others)
    arrived = [moved(grads[offset], offset) for offset in range(1, RING)]
    done = pl.pallas_call(
        sum_kernel,
        out_shape=shape(*done.shape),
        in_specs=[ANY] + [VMEM] * RING,
        out_specs=VMEM,
        input_output_aliases={0: 0},
        compiler_params=params,
    )(done, grads[0], *arrived)
    back = lax.all_to_all(done, both, 0, 0, axis_index_groups=heads_over)

    line = jnp.sum(back[:, -LOG_ROWS:-LOG_ROWS + 3, :].astype(f32), axis=(0, 1))
    dp = lax.axis_size("dp")
    terms = [lax.ppermute(line, "dp", [(i, i ^ s) for i in range(dp)]) for s in range(1, dp)]

    attended, dq, dk, dv = pl.pallas_call(
        after_kernel,
        out_shape=(shape(rows, width), shape(rows, width), shape(rows, kv_width), shape(rows, kv_width)),
        in_specs=[VMEM] * 3,
        out_specs=[VMEM] * 4,
        compiler_params=params,
    )(back, cosine, sine)

    level = [line] + terms
    while len(level) > 1:
        level = [a + b for a, b in zip(level[0::2], level[1::2])]
    line = level[0]
    base = ROPE_BASE ** (-(jnp.arange(HALF, dtype=f32) * 2.0 / HEAD))
    onehot = (index[0][:, None] == jnp.arange(table.shape[1], dtype=jnp.int32)[None, :]).astype(f32)
    log_factor = jnp.sum(onehot * table[0][None, :], axis=1)
    log_gradient = (line[:HALF] - line[HALF:]) * base * jnp.exp(-log_factor)
    table_grad = jnp.sum(onehot * log_gradient[:, None], axis=0) / (tokens * dp)
    return attended[None, None], dq[None, None], dk[None, None], dv[None, None], table_grad[None, :]


def solution(mesh):
    block = P("pipe", "dp", "ctx", None)
    return jax.shard_map(
        on_device,
        mesh=mesh,
        in_specs=(block,) * 5 + (P(), P("pipe", None), P("pipe", None)),
        out_specs=(block,) * 4 + (P("pipe", None),),
        check_vma=False,
    )
```

```python
import math

import jax
import jax.numpy as jnp
from jax import lax
from jax.experimental import pallas as pl
from jax.experimental.pallas import tpu as pltpu
from jax.sharding import PartitionSpec as P

HEAD = 128
HALF = 64
ROPE_BASE = 500000.0
LOG_ROWS = 16
TILE = 512
RING = 4
LOG2E = math.log2(math.e)

VMEM = pl.BlockSpec(memory_space=pltpu.VMEM)
SMEM = pl.BlockSpec(memory_space=pltpu.SMEM)
ANY = pl.BlockSpec(memory_space=pl.ANY)
HBM = pl.BlockSpec(memory_space=pltpu.HBM)
f32 = jnp.float32
bf16 = jnp.bfloat16


def dot(a, b):
    return jnp.dot(a, b, preferred_element_type=f32)


def dot_nt(a, b):
    return lax.dot_general(a, b, (((1,), (1,)), ((), ())), preferred_element_type=f32)


def swap_halves(u):
    return pltpu.roll(u, HALF, 1)


def half_rates(table_ref, index_row):
    pair = lax.broadcasted_iota(jnp.int32, (1, HALF), 1).astype(f32)
    log_factor = jnp.zeros((1, HALF), f32)
    for entry in range(table_ref.shape[1]):
        log_factor = jnp.where(index_row == entry, table_ref[0, entry], log_factor)
    return jnp.exp(-pair * (2.0 / HEAD * math.log(ROPE_BASE)) - log_factor)


def first_kernel(order_hbm, table_hbm, index_hbm, k_hbm, v_hbm,
                 out_hbm, cos_hbm, sin_hbm,
                 order_ref, table_ref, index_ref, k_ref, v_ref, packed_k, cos_ref, sin_ref,
                 in_sems, v_sems, k_sems, wave_sems):
    rows = k_ref.shape[0]
    half_rows = rows // 2
    kv_heads = k_ref.shape[1] // HEAD
    start = out_hbm.shape[1] - 2 * rows
    pairs = ((order_hbm, order_ref), (table_hbm, table_ref), (index_hbm, index_ref), (k_hbm, k_ref), (v_hbm, v_ref))
    copies = [pltpu.make_async_copy(a, b, in_sems.at[i]) for i, (a, b) in enumerate(pairs)]
    for copy in copies:
        copy.start()
    sent = []

    def send(source, to, sem):
        copy = pltpu.make_async_copy(source, to, sem)
        copy.start()
        sent.append(copy)

    for copy in copies[:3]:
        copy.wait()
    me = lax.axis_index("ctx")
    rate = half_rates(table_ref, index_ref[...])
    row = lax.broadcasted_iota(jnp.int32, (rows, HALF), 0)
    first, second = order_ref[2 * me] * half_rows, order_ref[2 * me + 1] * half_rows
    position = jnp.where(row < half_rows, first + row, second + row - half_rows).astype(f32)
    angle = position * rate
    cosine = jnp.cos(angle)
    sine = jnp.sin(angle)
    cosine = jnp.concatenate([cosine, cosine], axis=1)
    signed = jnp.concatenate([-sine, sine], axis=1)
    cos_ref[...] = cosine
    sin_ref[...] = signed
    send(cos_ref, cos_hbm, wave_sems.at[0])
    send(sin_ref, sin_hbm, wave_sems.at[1])
    copies[3].wait()
    copies[4].wait()
    for kv in range(kv_heads):
        cols = slice(kv * HEAD, (kv + 1) * HEAD)
        send(v_ref.at[:, pl.ds(kv * HEAD, HEAD)], out_hbm.at[kv, pl.ds(start + rows, rows), :], v_sems.at[kv])
        u = k_ref[:, cols].astype(f32)
        packed_k[kv] = (u * cosine + swap_halves(u) * signed).astype(bf16)
        send(packed_k.at[kv], out_hbm.at[kv, pl.ds(start, rows), :], k_sems.at[kv])
    for copy in sent:
        copy.wait()


def second_kernel(held_hbm, cos_hbm, sin_hbm, q_hbm, prior_hbm, do_hbm, out_hbm,
                  cos_ref, sin_ref, q_ref, prior_ref, do_ref, packed_q, in_sems, do_sems, q_sems):
    rows, width = q_ref.shape
    heads = width // HEAD
    group = heads // out_hbm.shape[0]
    copies = [pltpu.make_async_copy(cos_hbm, cos_ref, in_sems.at[0]), pltpu.make_async_copy(sin_hbm, sin_ref, in_sems.at[1])]
    for kv in range(heads // group):
        cols = pl.ds(kv * group * HEAD, group * HEAD)
        for a, b in ((q_hbm, q_ref), (prior_hbm, prior_ref), (do_hbm, do_ref)):
            copies.append(pltpu.make_async_copy(a.at[:, cols], b.at[:, cols], in_sems.at[len(copies)]))
    for copy in copies:
        copy.start()
    sent = []

    def send(source, head, part, sem):
        to = out_hbm.at[head // group, pl.ds((part * group + head % group) * rows, rows), :]
        copy = pltpu.make_async_copy(source, to, sem)
        copy.start()
        sent.append(copy)

    for copy in copies[:2]:
        copy.wait()
    cosine, signed = cos_ref[...], sin_ref[...]
    for head in range(heads):
        cols = slice(head * HEAD, (head + 1) * HEAD)
        if head % group == 0:
            for copy in copies[2 + 3 * (head // group):5 + 3 * (head // group)]:
                copy.wait()
        u = q_ref[:, cols].astype(f32) + prior_ref[:, cols].astype(f32)
        packed_q[head] = (u * cosine + swap_halves(u) * signed).astype(bf16)
        send(packed_q.at[head], head, 0, q_sems.at[head])
        send(do_ref.at[:, pl.ds(head * HEAD, HEAD)], head, 1, do_sems.at[head])
    for copy in sent:
        copy.wait()


def placed_at():
    chip = lax.axis_index("ctx")
    core = lax.axis_index("pipe")
    row, column = chip // RING, chip % RING
    return core == 0, jnp.where(core == 0, row, column), jnp.where(core == 0, column, row)


def main_kernel(order_ref, in_ref, own_ref, next_ref, far_ref, last_ref,
                out_ref, grad_own, grad_next, grad_far, grad_last,
                qs, dos, ks, vs, kt, vt, dk, dv, atts, dqs, s_scr, e_scr, ds_scr, angle_ref, place_ref):
    rows = own_ref.shape[1] // 2
    half_rows = rows // 2
    group = in_ref.shape[1] // rows // 2 - 1
    tokens = ks.shape[0]
    block = group * half_rows
    scale = HEAD ** -0.5
    coef = scale * LOG2E
    straight, _, column = placed_at()

    def slot_of(rank, offset, half):
        at = lax.rem(column + offset, RING)
        return order_ref[2 * jnp.where(straight, rank * RING + at, at * RING + rank) + half]

    def half_block(ref, number):
        return ref.at[pl.ds(pl.multiple_of(number * half_rows, half_rows), half_rows), :]

    pieces = [(rank, half) for rank in range(RING) for half in range(2)]
    keys_of = [own_ref, next_ref, far_ref, last_ref]
    for offset, ref in enumerate(keys_of):
        for rank, half in pieces:
            number = slot_of(rank, offset, half)
            half_block(ks, number)[...] = ref[rank, half * half_rows:(half + 1) * half_rows, :]
            half_block(vs, number)[...] = ref[rank, rows + half * half_rows:rows + (half + 1) * half_rows, :]
    places = [slot_of(rank, 0, half) for rank, half in pieces]
    ranks = []
    for place in places:
        above = jnp.int32(0)
        for other in places:
            above = above + jnp.where(other < place, 1, 0)
        ranks.append(above)
        place_ref[above] = place
    for (rank, half), at in zip(pieces, ranks):
        for head in range(group):
            start = head * rows + half * half_rows
            half_block(qs, at * group + head)[...] = in_ref[rank, start:start + half_rows, :]
            start = start + group * rows
            half_block(dos, at * group + head)[...] = in_ref[rank, start:start + half_rows, :]
    kt[...] = ks[...].T
    vt[...] = vs[...].T
    dk[...] = jnp.zeros_like(dk)
    dv[...] = jnp.zeros_like(dv)
    angle_ref[...] = jnp.zeros_like(angle_ref)

    key_iota = lax.broadcasted_iota(jnp.int32, (TILE, TILE), 0)
    lane = lax.broadcasted_iota(jnp.int32, (1, TILE), 1)
    line = lax.broadcasted_iota(jnp.int32, (TILE, 1), 0)
    row_number = lax.broadcasted_iota(jnp.int32, (TILE, HEAD), 0)

    def weighted(gradient, rotated, position):
        term = gradient * swap_halves(rotated.astype(f32)) * position
        return jnp.sum(term.reshape(TILE // 8, 8, HEAD), axis=0)

    def query_places(m):
        return place_ref[2 * m] * half_rows, place_ref[2 * m + 1] * half_rows

    def tile_of(m):
        return pl.ds(pl.multiple_of(m * TILE, TILE), TILE)

    def scores(m, chunks, buffer):
        low, high = query_places(m)
        q = qs[tile_of(m), :]
        position = jnp.where(lane < block, low, high) + lax.rem(lane, half_rows)
        top = None
        for c in range(chunks):
            keys = slice(c * TILE, (c + 1) * TILE)
            s = dot_nt(ks[keys, :], q)
            s = jnp.where(key_iota <= position - c * TILE, s, -1e30)
            s_scr[buffer, keys, :] = s
            peak = jnp.max(s, axis=0, keepdims=True)
            top = peak if top is None else jnp.maximum(top, peak)
        return top * coef

    def forward(m, chunks, buffer, top):
        tile = tile_of(m)
        seen = chunks * TILE
        total = jnp.zeros((1, TILE), f32)
        for c in range(chunks):
            keys = slice(c * TILE, (c + 1) * TILE)
            e = jnp.exp2(s_scr[buffer, keys, :] * coef - top)
            total = total + jnp.sum(e, axis=0, keepdims=True)
            e_scr[buffer, keys, :] = e.astype(bf16)
        inverse = 1.0 / total
        o_t = dot(vt[:, :seen], e_scr[buffer, :seen, :]) * inverse
        atts[tile, :] = o_t.T.astype(bf16)
        do_t = (dos[tile, :].T.astype(f32) * inverse).astype(bf16)
        delta = jnp.sum(do_t.astype(f32) * o_t, axis=0, keepdims=True)
        return do_t, delta

    def backward(m, chunks, buffer, do_t, delta):
        low, high = query_places(m)
        tile = tile_of(m)
        seen = chunks * TILE
        q = qs[tile, :]
        do = do_t.T
        for c in range(chunks):
            keys = slice(c * TILE, (c + 1) * TILE)
            e = e_scr[buffer, keys, :]
            dv[keys, :] += dot(e, do)
            dp = dot(vs[keys, :], do_t)
            ds = (e.astype(f32) * (dp - delta)).astype(bf16)
            ds_scr[buffer, keys, :] = ds
            dk[keys, :] += dot(ds, q)
        gq = (dot(kt[:, :seen], ds_scr[buffer, :seen, :]) * scale).T
        dqs[tile, :] = gq.astype(bf16)
        at = (jnp.where(line < block, low, high) + lax.rem(line, half_rows)).astype(f32)
        angle_ref[...] += weighted(gq, q, at)

    def attend(m, few, many):
        top = scores(2 * m, few, 0)
        first = forward(2 * m, few, 0, top)
        top = scores(2 * m + 1, many, 1)
        backward(2 * m, few, 0, *first)
        second = forward(2 * m + 1, many, 1, top)
        backward(2 * m + 1, many, 1, *second)

    def two_tiles(m, carry):
        few = place_ref[4 * m + 1] * half_rows // TILE
        many = place_ref[4 * m + 3] * half_rows // TILE
        last = tokens // TILE
        steps = jnp.maximum(many, few + 1)
        for n in range(1, last):
            @pl.when(jnp.maximum(steps, 1) == n)
            def _():
                attend(m, n, n + 1)

        @pl.when(steps == last)
        def _():
            attend(m, last, last)
        return carry

    lax.fori_loop(0, qs.shape[0] // TILE // 2, two_tiles, 0)

    for i in range(tokens // TILE):
        tile = slice(i * TILE, (i + 1) * TILE)
        gk = dk[tile, :] * scale
        dk[tile, :] = gk
        angle_ref[...] += weighted(gk, ks[tile, :], (row_number + i * TILE).astype(f32))

    for (rank, half), at in zip(pieces, ranks):
        for head in range(group):
            start = head * rows + half * half_rows
            out_ref[rank, start:start + half_rows, :] = half_block(atts, at * group + head)[...]
            start = start + group * rows
            out_ref[rank, start:start + half_rows, :] = half_block(dqs, at * group + head)[...]
    packed = split_line(jnp.sum(angle_ref[...], axis=0, keepdims=True))
    for offset, ref in enumerate((grad_own, grad_next, grad_far, grad_last)):
        for rank, half in pieces:
            number = slot_of(rank, offset, half)
            start = half * half_rows
            ref[rank, start:start + half_rows, :] = half_block(dk, number)[...].astype(bf16)
            ref[rank, rows + start:rows + start + half_rows, :] = half_block(dv, number)[...].astype(bf16)
        for rank in range(RING):
            ref[rank, 2 * rows:, :] = packed


def split_line(line):
    high = line.astype(bf16).astype(f32)
    middle = (line - high).astype(bf16).astype(f32)
    low = line - high - middle
    which = lax.broadcasted_iota(jnp.int32, (LOG_ROWS, HEAD), 0)
    packed = jnp.where(which == 0, high, jnp.where(which == 1, middle, jnp.where(which == 2, low, 0.0)))
    return packed.astype(bf16)


def sum_kernel(held_ref, own_ref, next_ref, far_ref, last_ref, out_ref):
    grads = (own_ref, next_ref, far_ref, last_ref)
    size = own_ref.shape[1] - LOG_ROWS
    start = out_ref.shape[1] - LOG_ROWS - size
    for rank in range(RING):
        total = grads[0][rank, :size].astype(f32)
        for ref in grads[1:]:
            total = total + ref[rank, :size].astype(f32)
        out_ref[rank, start:start + size, :] = total.astype(bf16)
    _, _, column = placed_at()
    lines = [jnp.sum(ref[0, size:].astype(f32), axis=0, keepdims=True) for ref in grads]
    line = jnp.zeros((1, HEAD), f32)
    for at in range(RING):
        offset = lax.rem(column - at + RING, RING)
        term = lines[0]
        for number in range(1, RING):
            term = jnp.where(offset == number, lines[number], term)
        line = line + term
    packed = split_line(line)
    for rank in range(RING):
        out_ref[rank, start + size:, :] = packed


def after_kernel(in_ref, cos_ref, sin_ref, att_ref, dq_ref, dk_ref, dv_ref):
    rows = cos_ref.shape[0]
    group = att_ref.shape[1] // dk_ref.shape[1]
    cosine, signed = cos_ref[...], sin_ref[...]

    def back(u):
        u = u.astype(f32)
        return (u * cosine - swap_halves(u) * signed).astype(bf16)

    for kv in range(RING):
        for number in range(group):
            head = kv * group + number
            cols = slice(head * HEAD, (head + 1) * HEAD)
            att_ref[:, cols] = in_ref[kv, number * rows:(number + 1) * rows]
            dq_ref[:, cols] = back(in_ref[kv, (group + number) * rows:(group + number + 1) * rows])
        cols = slice(kv * HEAD, (kv + 1) * HEAD)
        start = 2 * group * rows
        dk_ref[:, cols] = back(in_ref[kv, start:start + rows])
        dv_ref[:, cols] = in_ref[kv, start + rows:start + 2 * rows]


def shape(*dims, dtype=bf16):
    return jax.ShapeDtypeStruct(dims, dtype)


def on_device(queries, key_rows, values, prior, later, order, table, index):
    rows, width = queries.shape[2:]
    kv_width = key_rows.shape[3]
    heads = width // HEAD
    sources = lax.axis_size("ctx")
    pipe = lax.axis_size("pipe")
    tokens = rows * sources
    group = width // kv_width
    arriving = lax.ppermute(prior, "pipe", [(i, (i + 1) % pipe) for i in range(pipe)])
    returning = lax.ppermute(later, "pipe", [(i, (i - 1) % pipe) for i in range(pipe)])
    params = pltpu.CompilerParams(vmem_limit_bytes=40 * 2**20)
    both = ("pipe", "ctx")

    def device(core, rank, column):
        return core * sources + (rank * RING + column if core == 0 else column * RING + rank)

    heads_over = [[device(core, rank, column) for rank in range(RING)]
                  for core in range(pipe) for column in range(RING)]

    def moved(value, by):
        pairs = [(device(core, rank, column), device(core, rank, (column + by) % RING))
                 for core in range(pipe) for rank in range(RING) for column in range(RING)]
        return lax.ppermute(value, both, pairs)

    payload = shape(RING, 2 * (group + 1) * rows, HEAD)
    wave = shape(rows, HEAD, dtype=f32)
    wide = pltpu.CompilerParams(vmem_limit_bytes=56 * 2**20)
    wave_buffer = pltpu.VMEM((rows, HEAD), f32)
    kv_buffer = pltpu.VMEM((rows, kv_width), bf16)
    buffer = pltpu.VMEM((rows, width), bf16)
    sent, cosine, sine = pl.pallas_call(
        first_kernel,
        out_shape=(payload, wave, wave),
        in_specs=[HBM] * 5,
        out_specs=[HBM] * 3,
        scratch_shapes=[
            pltpu.SMEM(order.shape, jnp.int32),
            pltpu.SMEM(table.shape, f32),
            pltpu.VMEM(index.shape, jnp.int32),
            kv_buffer,
            kv_buffer,
            pltpu.VMEM((RING, rows, HEAD), bf16),
            wave_buffer,
            wave_buffer,
            pltpu.SemaphoreType.DMA((5,)),
            pltpu.SemaphoreType.DMA((RING,)),
            pltpu.SemaphoreType.DMA((RING,)),
            pltpu.SemaphoreType.DMA((2,)),
        ],
        compiler_params=wide,
        cost_estimate=pl.CostEstimate(flops=10**7, bytes_accessed=4 * 10**6, transcendentals=0),
    )(order, table, index, key_rows[0, 0], values[0, 0])
    sent = pl.pallas_call(
        second_kernel,
        out_shape=payload,
        in_specs=[HBM] * 6,
        out_specs=HBM,
        scratch_shapes=[wave_buffer, wave_buffer, buffer, buffer, buffer, pltpu.VMEM((heads, rows, HEAD), bf16)]
        + [pltpu.SemaphoreType.DMA((2 + 3 * RING,))] + [pltpu.SemaphoreType.DMA((heads,))] * 2,
        input_output_aliases={0: 0},
        compiler_params=wide,
    )(sent, cosine, sine, queries[0, 0], arriving[0, 0], returning[0, 0])

    held = lax.all_to_all(sent, both, 0, 0, axis_index_groups=heads_over)
    own = held[:, 2 * group * rows:, :]
    others = [moved(own, RING - offset) for offset in range(1, RING)]

    grads = shape(RING, 2 * rows + LOG_ROWS, HEAD)
    done, *grads = pl.pallas_call(
        main_kernel,
        out_shape=[shape(RING, 2 * (group + 1) * rows + LOG_ROWS, HEAD)] + [grads] * RING,
        in_specs=[SMEM] + [VMEM] * (1 + RING),
        out_specs=[VMEM] * (1 + RING),
        scratch_shapes=[pltpu.VMEM((tokens, HEAD), bf16)] * 4
        + [pltpu.VMEM((HEAD, tokens), bf16)] * 2
        + [pltpu.VMEM((tokens, HEAD), f32)] * 2
        + [pltpu.VMEM((tokens, HEAD), bf16)] * 2
        + [pltpu.VMEM((2, tokens, TILE), f32)]
        + [pltpu.VMEM((2, tokens, TILE), bf16)] * 2
        + [pltpu.VMEM((8, HEAD), f32), pltpu.SMEM((2 * RING,), jnp.int32)],
        compiler_params=params,
    )(order, held, own, *others)
    arrived = [moved(grads[offset], offset) for offset in range(1, RING)]
    done = pl.pallas_call(
        sum_kernel,
        out_shape=shape(*done.shape),
        in_specs=[ANY] + [VMEM] * RING,
        out_specs=VMEM,
        input_output_aliases={0: 0},
        compiler_params=params,
    )(done, grads[0], *arrived)
    back = lax.all_to_all(done, both, 0, 0, axis_index_groups=heads_over)

    line = jnp.sum(back[:, -LOG_ROWS:-LOG_ROWS + 3, :].astype(f32), axis=(0, 1))
    dp = lax.axis_size("dp")
    terms = [lax.ppermute(line, "dp", [(i, i ^ s) for i in range(dp)]) for s in range(1, dp)]

    attended, dq, dk, dv = pl.pallas_call(
        after_kernel,
        out_shape=(shape(rows, width), shape(rows, width), shape(rows, kv_width), shape(rows, kv_width)),
        in_specs=[VMEM] * 3,
        out_specs=[VMEM] * 4,
        compiler_params=params,
    )(back, cosine, sine)

    level = [line] + terms
    while len(level) > 1:
        level = [a + b for a, b in zip(level[0::2], level[1::2])]
    line = level[0]
    base = ROPE_BASE ** (-(jnp.arange(HALF, dtype=f32) * 2.0 / HEAD))
    onehot = (index[0][:, None] == jnp.arange(table.shape[1], dtype=jnp.int32)[None, :]).astype(f32)
    log_factor = jnp.sum(onehot * table[0][None, :], axis=1)
    log_gradient = (line[:HALF] - line[HALF:]) * base * jnp.exp(-log_factor)
    table_grad = jnp.sum(onehot * log_gradient[:, None], axis=0) / (tokens * dp)
    return attended[None, None], dq[None, None], dk[None, None], dv[None, None], table_grad[None, :]


def solution(mesh):
    block = P("pipe", "dp", "ctx", None)
    return jax.shard_map(
        on_device,
        mesh=mesh,
        in_specs=(block,) * 5 + (P(), P("pipe", None), P("pipe", None)),
        out_specs=(block,) * 4 + (P("pipe", None),),
        check_vma=False,
    )
```
